128 devices in a mesh: bins: 4 (over z_lo, core), nuis: 32 (over x, y, z_hi).
Axes of the slice: x: 4, y: 4, z: 4 (z_hi: 2, z_lo: 2; z = z_hi * 2 + z_lo), core: 2. Of those that a mesh axis runs over, the one named last changes fastest.
Arguments:
- log_kappa: bfloat16 [6144, 8192], P('bins', 'nuis'), may hold values from -0.0390625 to 0.0390625
- block_mask: int32 [48, 8192], P('bins', 'nuis'), may hold values 0 or 1
- process: int32 [48], P('bins'), may hold values from 0 to 7
- channel: int32 [48], P('bins'), may hold values from 0 to 3
- nominal: float32 [6144], P('bins'), may hold values from 1 to 10
- observed: float32 [6144], P('bins'), may hold values from 1 to 20
- process_rate: float32 [8], replicated, may hold values from 0.5 to 2
- efficiency: float32 [4], replicated, may hold values from 0.4 to 1.6
- nuisance_pulls: float32 [8192], P('nuis'), may hold values from -5 to 5
- impact_rhs: float32 [8192, 256], P('nuis'), may hold values from -6 to 6
Outputs:
- gradient: float32 [8192], P('nuis')
- hessian: float32 [8192, 8192], P('bins', 'nuis')
- impacts: float32 [8192, 256], P('nuis')
- residual: float32 [8192, 256], P('nuis')
The draws below stay inside these ranges and needn't reach their ends.
All inputs are finite; a program needn't handle non-finite values. No bound on the sum of `block_mask` on one device may be relied on, other than what follows from the above.
Results may differ from the reference program's by a relative error of at most 0.0029.
Values may be sent and summed in bfloat16 or wider, within the bound.
A program may use at most 128 MiB of HBM per device.

```python
import math
import jax
import jax.numpy as jnp
from jax import lax

BLK = 128
NUIS = 8192
IMP = 256
PROC = 8
CHAN = 4
BINS = 6144
BLOCKS = 48


def place_ends(values, own_key, least, high):
    extent = values.shape
    place = [jax.random.randint(jax.random.fold_in(own_key, axis), (), 0, extent[axis]) for axis in range(len(extent))]
    values = values.at[tuple(place)].set(least)
    longest = extent.index(max(extent))
    place[longest] = (place[longest] + 1) % extent[longest]
    return values.at[tuple(place)].set(high)


def levels(key, dims, pieces, least, largest):
    gain, own = 1.0, jax.random.fold_in(key, 6)
    for axis_at, shards_of in pieces:
        draws = jnp.exp(jax.random.uniform(jax.random.fold_in(own, axis_at), (shards_of,), jnp.float32, least / len(pieces), largest / len(pieces)))
        gain = gain * jnp.repeat(draws, dims[axis_at] // shards_of).reshape([-1 if axis == axis_at else 1 for axis in range(len(dims))])
    return gain


def gaussian(own_key, shape, deviation, reach, pieces=(), kind=jnp.bfloat16):
    result = jax.random.normal(own_key, shape, jnp.float32) * deviation
    if len(pieces) > 0:
        result = levels(own_key, shape, pieces, -0.22, 0.18) * result
    return jnp.clip(result, min=-reach, max=reach).astype(kind)


def setup_inputs(seed: int = 0) -> dict:
    streams_of = jax.random.split(jax.random.key(seed), 11)
    return {
        "log_kappa": gaussian(streams_of[0], (BINS, NUIS), (4 * BINS) ** -0.5, 0.0390625, ((0, 4), (1, 32))),
        "block_mask": place_ends((jax.random.randint(streams_of[1], (BLOCKS, NUIS), 0, 4) < 3).astype(jnp.int32), jax.random.fold_in(streams_of[1], 1), 0, 1),
        "process": place_ends(jax.random.randint(streams_of[2], (BLOCKS,), 0, PROC), jax.random.fold_in(streams_of[2], 1), 0, PROC - 1).astype(jnp.int32),
        "channel": place_ends(jax.random.randint(streams_of[3], (BLOCKS,), 0, CHAN), jax.random.fold_in(streams_of[3], 1), 0, CHAN - 1).astype(jnp.int32),
        "nominal": jnp.clip(jnp.exp(math.log(10.0) - 2.3025851 * jax.random.uniform(streams_of[4], (BINS,), jnp.float32) ** levels(streams_of[4], (BINS,), ((0, 4),), -0.2, 0.2)), 1.0, 10.0),
        "observed": jnp.clip(jnp.exp(math.log(20.0) - 2.9957323 * jax.random.uniform(streams_of[5], (BINS,), jnp.float32) ** levels(streams_of[5], (BINS,), ((0, 4),), -0.2, 0.2)), 1.0, 20.0),
        "process_rate": jnp.clip(jnp.exp(jax.random.uniform(streams_of[6], (PROC,), jnp.float32, math.log(0.5), math.log(2.0))), 0.5, 2.0),
        "efficiency": jnp.clip(jnp.exp(jax.random.uniform(streams_of[7], (CHAN,), jnp.float32, math.log(0.4), math.log(1.6))), 0.4, 1.6),
        "nuisance_pulls": gaussian(streams_of[8], (NUIS,), 1.0, 5.0, ((0, 32),), jnp.float32),
        "impact_rhs": gaussian(streams_of[9], (NUIS, IMP), 1.0, 6.0, ((0, 32),), jnp.float32),
    }


def solve_spd(curvature, gram_rr):
    factor_low = jnp.linalg.cholesky(curvature)
    halfway = lax.linalg.triangular_solve(factor_low, gram_rr, left_side=True, lower=True)
    return lax.linalg.triangular_solve(factor_low, halfway, left_side=True, lower=True, transpose_a=True)

def reference(log_kappa, block_mask, process, channel, nominal, observed, process_rate, efficiency, nuisance_pulls, impact_rhs):
    highest = lax.Precision.HIGHEST
    morph_kappa = (log_kappa.reshape(BLOCKS, BLK, NUIS) * block_mask[:, None, :].astype(jnp.bfloat16)).reshape(BINS, NUIS)
    kappa_wide = morph_kappa.astype(jnp.float32)
    exponent = jnp.dot(kappa_wide, nuisance_pulls, precision=highest)
    process_hot = (process[:, None] == jnp.arange(PROC)[None, :]).astype(jnp.float32)
    channel_hot = (channel[:, None] == jnp.arange(CHAN)[None, :]).astype(jnp.float32)
    block_scale = jnp.dot(process_hot, process_rate, precision=highest) * jnp.dot(channel_hot, efficiency, precision=highest)
    yields = nominal * jnp.repeat(block_scale, BLK) * jnp.exp(exponent)
    gradient = jnp.dot(yields - observed, kappa_wide, precision=highest) + nuisance_pulls
    weighted = (yields[:, None] * kappa_wide).astype(jnp.bfloat16)
    hessian = lax.dot_general(morph_kappa.astype(jnp.float32), weighted.astype(jnp.float32), (((0,), (0,)), ((), ())), preferred_element_type=jnp.float32)
    hessian = hessian + jnp.eye(NUIS, dtype=jnp.float32)
    image = lax.dot_general(hessian, impact_rhs, (((0,), (0,)), ((), ())), precision=highest)
    gram_rr = lax.dot_general(impact_rhs, impact_rhs, (((0,), (0,)), ((), ())), precision=highest)
    raw_curv = lax.dot_general(impact_rhs, image, (((0,), (0,)), ((), ())), precision=highest)
    curvature = 0.5 * (raw_curv + raw_curv.T)
    newton_step = solve_spd(curvature, gram_rr)
    impacts = jnp.dot(impact_rhs, newton_step, precision=highest)
    residual = impact_rhs - jnp.dot(image, newton_step, precision=highest)
    return (gradient, hessian, impacts, residual)
```

```python
import jax
import jax.numpy as jnp
from jax import lax
from jax.experimental import pallas as pl
from jax.experimental.pallas import tpu as pltpu
from jax.sharding import PartitionSpec as P

MESH = pl.DeviceIdType.MESH
F32, BF16 = jnp.float32, jnp.bfloat16
HIGHEST = lax.Precision.HIGHEST
ROWS, COLS, SHARE, PEERS = 1536, 256, 48, 32
HALF = ROWS // 2
PIV = 32


def dot0(a, b, precision=None):
    return lax.dot_general(
        a, b, (((0,), (0,)), ((), ())), preferred_element_type=F32, precision=precision
    )


def split2(v):
    hi = v.astype(BF16).astype(F32)
    return hi, (v - hi).astype(BF16).astype(F32)


def split3(v):
    hi, mid = split2(v)
    return hi, mid, (v - hi) - mid


def lanes3(v, lane):
    hi, mid, low = split3(v)
    return jnp.where(lane == 0, hi, jnp.where(lane == 1, mid, jnp.where(lane == 2, low, 0.0)))


def lane_of(rows, lanes=128):
    return lax.broadcasted_iota(jnp.int32, (rows, lanes), 1)


def invert(block):
    lane = lax.broadcasted_iota(jnp.int32, (PIV, PIV), 1)
    sub = lax.broadcasted_iota(jnp.int32, (PIV, PIV), 0)
    top = lax.broadcasted_iota(jnp.int32, (1, PIV), 1)
    for j in range(PIV):
        inv = 1.0 / block[j : j + 1, j : j + 1]
        row = jnp.where(top == j, inv, block[j : j + 1, :] * inv)
        rest = jnp.where(lane == j, 0.0, block)
        block = jnp.where(sub == j, row, rest - block[:, j : j + 1] * row)
    return block


def kernel(
    lk, mask, nom, obs, pul, rhs, proc, chan, rate, eff,
    grad_o, hess_o, imp_o, res_o,
    krow, kcol, wcol, sb, rb, fb, acol, ocol, ycol, vh, vl, dv, g3, g3r, c3, im, ab,
    pown, psend, precv, osend, orecv,
    a_s, a_r, b_s, b_r, k_s, k_r, x_s, x_r, e_s, e_r, o_s, o_r,
):
    n = lax.axis_index("nuis")
    b = lax.axis_index("bins")
    x, y, zh = n // 8, (n // 2) % 4, n % 2
    zl, core = b // 2, b % 2

    def dev(dx=0, dy=0, dz=0):
        return {"nuis": ((x + dx) % 4) * 8 + ((y + dy) % 4) * 2 + (zh + dz) % 2, "bins": b}

    def place(dy=0, dz=0):
        return ((y + dy) % 4) * 2 + (zh + dz) % 2

    def remote(src, dst, s, r, to):
        return pltpu.make_async_remote_copy(
            src_ref=src, dst_ref=dst, send_sem=s, recv_sem=r, device_id=to, device_id_type=MESH
        )

    own = place()
    core_mate = {"nuis": n, "bins": zl * 2 + (1 - core)}
    z_mate = {"nuis": n, "bins": (1 - zl) * 2 + core}

    def out_dev(t):
        return {"nuis": (2 * core + t) * 8 + y * 2 + zh, "bins": x}

    def out_is_self(t):
        return jnp.logical_and(2 * core + t == x, x == b)

    def in_dev(s):
        return {"nuis": b * 8 + y * 2 + zh, "bins": 2 * s + x // 2}

    def in_is_self(s):
        return jnp.logical_and(b == x, 2 * s + x // 2 == b)

    bar = pltpu.get_barrier_semaphore()

    def greet(k, carry):
        pl.semaphore_signal(
            bar, inc=1, device_id={"nuis": (n + k) % PEERS, "bins": b}, device_id_type=MESH
        )
        return carry

    lax.fori_loop(1, PEERS, greet, 0)
    for mate in (core_mate, z_mate):
        pl.semaphore_signal(bar, inc=1, device_id=mate, device_id_type=MESH)
    expected = jnp.int32(PEERS - 1 + 2)
    for t in range(2):
        for other, itself in ((out_dev(t), out_is_self(t)), (in_dev(t), in_is_self(t))):

            @pl.when(jnp.logical_not(itself))
            def _():
                pl.semaphore_signal(bar, inc=1, device_id=other, device_id_type=MESH)

            expected = expected + jnp.where(itself, 0, 1)

    rhs_v = rhs[...]
    r_hi, r_mid = split2(rhs_v)
    r_hi, r_mid = r_hi.astype(BF16), r_mid.astype(BF16)

    def own_rows(i, carry):
        at = pl.ds(pl.multiple_of(i * 128, 128), 128)
        lane = lane_of(128)
        kb = lk[at, :] * mask[pl.ds(i, 1), :].astype(F32).astype(BF16)
        krow[own, at, :] = kb
        kcol[x, at, :] = kb
        e = jnp.sum(kb.astype(F32) * pul[...], axis=1, keepdims=True)
        sb[at, 256:384] = lanes3(e, lane).astype(BF16)
        m = jnp.dot(kb, r_hi, preferred_element_type=F32) + jnp.dot(
            kb, r_mid, preferred_element_type=F32
        )
        sb[at, 0:256] = m.astype(BF16)
        scale = rate[proc[i]] * eff[chan[i]]
        acol[at, :] = jnp.transpose(jnp.broadcast_to(nom[pl.ds(i, 1), :] * scale, (128, 128)))
        ocol[at, :] = jnp.transpose(jnp.broadcast_to(obs[pl.ds(i, 1), :], (128, 128)))
        return carry

    lax.fori_loop(0, 12, own_rows, 0)

    gram = dot0(rhs_v, rhs_v, HIGHEST)
    for i, part in enumerate((gram[0:128, 0:128], gram[128:256, 0:128], gram[128:256, 128:256])):
        g3[128 * i : 128 * (i + 1), :] = part
        g3r[128 * i : 128 * (i + 1), :] = pltpu.roll(part, 64, 1)

    def put_gram(i, carry):
        at = pl.ds(pl.multiple_of(i * 24, 8), 24)
        for h, ref in enumerate((g3r, g3)):
            hi, low = split2(ref[at, :])
            piece = jnp.concatenate([hi, low], axis=0)
            piece = jnp.where(lane_of(SHARE) >= 64, piece, 0.0)
            to = pl.ds(pl.multiple_of((2 * i + h) * SHARE, 16), SHARE)
            sb[to, 256:384] = (sb[to, 256:384].astype(F32) + piece).astype(BF16)
        return carry

    lax.fori_loop(0, 16, put_gram, 0)

    pl.semaphore_wait(bar, expected)

    def sum_copy(k):
        to = (n + k) % PEERS
        return remote(
            sb.at[pl.ds(pl.multiple_of(to * SHARE, 16), SHARE)], rb.at[k], a_s.at[k], a_r.at[k],
            {"nuis": to, "bins": b},
        )

    def start_sum(k, carry):
        sum_copy(k).start()
        return carry

    lax.fori_loop(1, PEERS, start_sum, 0)

    def row_copy(i, slot, to, lo=0, size=ROWS):
        ref = krow.at[slot, pl.ds(lo, size)]
        return remote(ref, ref, k_s.at[i], k_r.at[i], to)

    def col_copy(i, slot, to, lo=0, size=ROWS):
        ref = kcol.at[slot, pl.ds(lo, size)]
        return remote(ref, ref, k_s.at[i], k_r.at[i], to)

    up_x, down_x = (x + 1) % 4, (x + 3) % 4
    far_x = (x + 2) % 4
    sends = {
        0: row_copy(0, own, dev(dy=1)),
        1: row_copy(1, own, dev(dy=3)),
        2: row_copy(2, own, dev(dz=1)),
        3: col_copy(3, x, dev(dx=1)),
        4: col_copy(4, x, dev(dx=3)),
        5: row_copy(5, place(3), dev(dy=1), 0, HALF),
        6: row_copy(6, place(1), dev(dy=3), HALF, HALF),
        7: row_copy(7, place(0, 1), dev(dy=1)),
        8: row_copy(8, place(0, 1), dev(dy=3)),
        9: row_copy(9, place(2), dev(dz=1)),
        10: col_copy(10, down_x, dev(dx=1), 0, HALF),
        11: col_copy(11, up_x, dev(dx=3), HALF, HALF),
    }
    arrivals = {
        0: row_copy(0, place(3), dev(dy=3)),
        1: row_copy(1, place(1), dev(dy=1)),
        2: row_copy(2, place(0, 1), dev(dz=1)),
        3: col_copy(3, down_x, dev(dx=3)),
        4: col_copy(4, up_x, dev(dx=1)),
        5: row_copy(5, place(2), dev(dy=3), 0, HALF),
        6: row_copy(6, place(2), dev(dy=1), HALF, HALF),
        7: row_copy(7, place(3, 1), dev(dy=3)),
        8: row_copy(8, place(1, 1), dev(dy=1)),
        9: row_copy(9, place(2, 1), dev(dz=1)),
        10: col_copy(10, far_x, dev(dx=3), 0, HALF),
        11: col_copy(11, far_x, dev(dx=1), HALF, HALF),
    }
    for i in range(5):
        sends[i].start()

    def wait_sum(k, acc):
        sum_copy(k).wait_recv()
        return acc + rb[k].astype(F32)

    mine = pl.ds(pl.multiple_of(n * SHARE, 16), SHARE)
    acc = lax.fori_loop(1, PEERS, wait_sum, sb[mine, :].astype(F32))
    lane = lane_of(SHARE)
    ext = acc[:, 256:384]
    e = jnp.sum(jnp.where(lane < 3, ext, 0.0), axis=1, keepdims=True)
    yields = acol[mine, :] * jnp.exp(e)
    fb[mine, 0:256] = acc[:, 0:256].astype(BF16)
    hi, low = split2(ext[0:24] + ext[24:48])
    tail = jnp.where(lane >= 64, jnp.concatenate([hi, low], axis=0), lanes3(yields, lane))
    fb[mine, 256:384] = tail.astype(BF16)

    def share_copy(k):
        return remote(
            fb.at[mine], fb.at[mine], b_s.at[k], b_r.at[k],
            {"nuis": (n + k) % PEERS, "bins": b},
        )

    def share_arrival(k):
        origin = (n + PEERS - k) % PEERS
        ref = fb.at[pl.ds(pl.multiple_of(origin * SHARE, 16), SHARE)]
        return remote(ref, ref, b_s.at[k], b_r.at[k], {"nuis": origin, "bins": b})

    def start_share(k, carry):
        share_copy(k).start()
        return carry

    lax.fori_loop(1, PEERS, start_share, 0)

    for arrived, forward in ((0, (5,)), (1, (6,)), (2, (7, 8)), (3, (10,)), (4, (11,))):
        arrivals[arrived].wait_recv()
        for i in forward:
            sends[i].start()

    def wait_share(k, carry):
        share_arrival(k).wait_recv()
        return carry

    lax.fori_loop(1, PEERS, wait_share, 0)

    def all_rows(i, carry):
        at = pl.ds(pl.multiple_of(i * 128, 128), 128)
        lane = lane_of(128)
        ext = fb[at, 256:384].astype(F32)
        yl = jnp.sum(jnp.where(lane < 3, ext, 0.0), axis=1, keepdims=True)
        yl = jnp.broadcast_to(yl, (128, 128))
        ycol[at, :] = yl
        dv[at, :] = lanes3(yl - ocol[at, :], lane).astype(BF16)
        for h in range(2):
            lanes = slice(128 * h, 128 * (h + 1))
            vh[at, lanes] = (yl * fb[at, lanes].astype(F32)).astype(BF16)
            vl[at, lanes] = (yl * krow[own, at, lanes].astype(F32)).astype(BF16)
        return carry

    lax.fori_loop(0, 12, all_rows, 0)

    w = fb[:, 0:256]
    curv = dot0(w, vh[...])
    for i, part in enumerate((curv[0:128, 0:128], curv[128:256, 0:128], curv[128:256, 128:256])):
        c3[0, 128 * i : 128 * (i + 1), :] = part
    c_core = remote(c3.at[0], c3.at[1], x_s.at[0], x_r.at[0], core_mate)
    c_core.start()
    kept = krow[own]
    im[0, 0:256, :] = dot0(vl[...], w)
    slope = dot0(dv[...], kept)
    im[0, 256:264, :] = jnp.broadcast_to(slope[0:1] + slope[1:2] + slope[2:3], (8, COLS))
    i_core = remote(im.at[0], im.at[1], x_s.at[1], x_r.at[1], core_mate)
    i_core.start()

    c_core.wait_recv()
    c3[2] = c3[0] + c3[1]
    c_z = remote(c3.at[2], c3.at[3], x_s.at[2], x_r.at[2], z_mate)
    c_z.start()
    i_core.wait_recv()
    im[2] = im[0] + im[1]
    i_z = remote(im.at[2], im.at[3], x_s.at[3], x_r.at[3], z_mate)
    i_z.start()

    arrivals[5].wait_recv()
    arrivals[6].wait_recv()
    sends[9].start()
    arrivals[10].wait_recv()
    arrivals[11].wait_recv()

    def weigh(i, carry):
        at = pl.ds(pl.multiple_of(i * 128, 128), 128)
        yl = ycol[at, :]
        yl = jnp.concatenate([yl, yl], axis=1)
        for t in range(4):
            kc = kcol[(2 * core + t) % 4, at, :].astype(F32)
            wcol[at, 256 * t : 256 * (t + 1)] = (yl * kc).astype(BF16)
        return carry

    lax.fori_loop(0, 12, weigh, 0)

    def slot_of(k):
        j = k % 4
        return place(j + j // 2 - 2 * (j // 3), k // 4)

    def half_copy(k):
        return remote(psend.at[k], precv.at[k], e_s.at[k], e_r.at[k], core_mate)

    def multiply(k, carry):
        lhs = krow[slot_of(k)]
        psend[k] = dot0(lhs, wcol[:, 512:1024])
        half_copy(k).start()
        pown[k] = dot0(lhs, wcol[:, 0:512])
        return carry

    def out_copy(k, t):
        return remote(osend.at[k, t], orecv.at[zl, k], o_s.at[k, t], o_r.at[zl, k], out_dev(t))

    def own_copy(k, t):
        return pltpu.make_async_copy(osend.at[k, t], orecv.at[zl, k], o_r.at[zl, k])

    def hand_out(k, carry):
        half_copy(k).wait_recv()
        for t in range(2):
            lanes = slice(256 * t, 256 * (t + 1))
            osend[k, t] = (pown[k, :, lanes] + precv[k, :, lanes]).astype(BF16)

            @pl.when(out_is_self(t))
            def _():
                own_copy(k, t).start()

            @pl.when(jnp.logical_not(out_is_self(t)))
            def _():
                out_copy(k, t).start()

        return carry

    lax.fori_loop(0, 5, multiply, 0)
    lax.fori_loop(0, 5, hand_out, 0)
    for i in (7, 8, 9):
        arrivals[i].wait_recv()
    lax.fori_loop(5, 8, multiply, 0)
    lax.fori_loop(5, 8, hand_out, 0)

    def put_back(i, carry):
        at = pl.ds(pl.multiple_of(i * 24, 8), 24)
        parts = []
        for h in range(2):
            piece = fb[pl.ds(pl.multiple_of((2 * i + h) * SHARE, 16), SHARE), 256:384].astype(F32)
            parts.append(piece[0:24] + piece[24:48])
        g3[at, :] = jnp.where(lane_of(24) < 64, pltpu.roll(parts[0], 64, 1), parts[1])
        return carry

    lax.fori_loop(0, 16, put_back, 0)
    c_z.wait_recv()
    total = c3[2] + c3[3] + g3[...]
    for left, blocks in ((0, total), (256, g3[...])):
        ab[0:128, left : left + 128] = blocks[0:128]
        ab[128:256, left : left + 128] = blocks[128:256]
        ab[0:128, left + 128 : left + 256] = jnp.transpose(blocks[128:256])
        ab[128:256, left + 128 : left + 256] = blocks[256:384]

    def eliminate(i, carry):
        pivot = invert(ab[0:PIV, 0:PIV])
        head = jnp.dot(pivot, ab[0:PIV, :], preferred_element_type=F32, precision=HIGHEST)
        rest = ab[PIV:256, :] - jnp.dot(
            ab[PIV:256, 0:PIV], head, preferred_element_type=F32, precision=HIGHEST
        )
        ab[0 : 256 - PIV, 0:256] = pltpu.roll(rest[:, 0:256], 256 - PIV, 1)
        ab[0 : 256 - PIV, 256:512] = rest[:, 256:512]
        ab[256 - PIV : 256, 0:256] = pltpu.roll(head[:, 0:256], 256 - PIV, 1)
        ab[256 - PIV : 256, 256:512] = head[:, 256:512]
        return carry

    lax.fori_loop(0, 256 // PIV, eliminate, 0)
    step = ab[:, 256:512]
    imp_o[...] = jnp.dot(rhs_v, step, preferred_element_type=F32, precision=HIGHEST)
    i_z.wait_recv()
    image = rhs_v + (im[2, 0:256, :] + im[3, 0:256, :])
    res_o[...] = rhs_v - jnp.dot(image, step, preferred_element_type=F32, precision=HIGHEST)
    grad_o[...] = im[2, 256:257, :] + im[3, 256:257, :] + pul[...]

    def finish(k, carry):
        for s in range(2):
            pltpu.make_async_copy(orecv.at[s, k], orecv.at[s, k], o_r.at[s, k]).wait()
        block = orecv[0, k].astype(F32) + orecv[1, k].astype(F32)
        at = pl.ds(pl.multiple_of(slot_of(k) * 256, 256), 256)
        r = lax.broadcasted_iota(jnp.int32, (256, COLS), 0)
        c = lax.broadcasted_iota(jnp.int32, (256, COLS), 1)
        here = jnp.logical_and(x == b, k == 0)
        hess_o[at, :] = block + jnp.where(jnp.logical_and(r == c, here), 1.0, 0.0)
        return carry

    lax.fori_loop(0, 8, finish, 0)

    def drain_small(k, carry):
        sum_copy(k).wait_send()
        share_copy(k).wait_send()
        return carry

    lax.fori_loop(1, PEERS, drain_small, 0)
    for i in range(12):
        sends[i].wait_send()
    for copy in (c_core, c_z, i_core, i_z):
        copy.wait_send()

    def drain_blocks(k, carry):
        half_copy(k).wait_send()
        for t in range(2):

            @pl.when(jnp.logical_not(out_is_self(t)))
            def _():
                out_copy(k, t).wait_send()

        return carry

    lax.fori_loop(0, 8, drain_blocks, 0)


def body(
    log_kappa, block_mask, process, channel, nominal, observed, process_rate, efficiency,
    nuisance_pulls, impact_rhs,
):
    vmem = pl.BlockSpec(memory_space=pltpu.VMEM)
    smem = pl.BlockSpec(memory_space=pltpu.SMEM)
    dma = pltpu.SemaphoreType.DMA
    gradient, hessian, impacts, residual = pl.pallas_call(
        kernel,
        name="gauss_newton",
        out_shape=(
            jax.ShapeDtypeStruct((1, COLS), F32),
            jax.ShapeDtypeStruct((2048, COLS), F32),
            jax.ShapeDtypeStruct((256, 256), F32),
            jax.ShapeDtypeStruct((256, 256), F32),
        ),
        in_specs=[vmem] * 6 + [smem] * 4,
        out_specs=(vmem,) * 4,
        scratch_shapes=[
            pltpu.VMEM((8, ROWS, COLS), BF16),
            pltpu.VMEM((4, ROWS, COLS), BF16),
            pltpu.VMEM((ROWS, 1024), BF16),
            pltpu.VMEM((ROWS, 384), BF16),
            pltpu.VMEM((PEERS, SHARE, 384), BF16),
            pltpu.VMEM((ROWS, 384), BF16),
            pltpu.VMEM((ROWS, 128), F32),
            pltpu.VMEM((ROWS, 128), F32),
            pltpu.VMEM((ROWS, 128), F32),
            pltpu.VMEM((ROWS, 256), BF16),
            pltpu.VMEM((ROWS, 256), BF16),
            pltpu.VMEM((ROWS, 128), BF16),
            pltpu.VMEM((384, 128), F32),
            pltpu.VMEM((384, 128), F32),
            pltpu.VMEM((4, 384, 128), F32),
            pltpu.VMEM((4, 264, COLS), F32),
            pltpu.VMEM((256, 512), F32),
            pltpu.VMEM((8, 256, 512), F32),
            pltpu.VMEM((8, 256, 512), F32),
            pltpu.VMEM((8, 256, 512), F32),
            pltpu.VMEM((8, 2, 256, 256), BF16),
            pltpu.VMEM((2, 8, 256, 256), BF16),
            dma((PEERS,)), dma((PEERS,)), dma((PEERS,)), dma((PEERS,)),
            dma((12,)), dma((12,)), dma((4,)), dma((4,)),
            dma((8,)), dma((8,)), dma((8, 2)), dma((2, 8)),
        ],
        compiler_params=pltpu.CompilerParams(
            collective_id=0, has_side_effects=True, vmem_limit_bytes=60 * 2**20
        ),
    )(
        log_kappa, block_mask, nominal.reshape(12, 128), observed.reshape(12, 128),
        nuisance_pulls.reshape(1, COLS), impact_rhs, process, channel, process_rate, efficiency,
    )
    return gradient.reshape(COLS), hessian, impacts, residual


def solution(mesh):
    in_specs = (
        P("bins", "nuis"),
        P("bins", "nuis"),
        P("bins"),
        P("bins"),
        P("bins"),
        P("bins"),
        P(),
        P(),
        P("nuis"),
        P("nuis", None),
    )
    out_specs = (P("nuis"), P("bins", "nuis"), P("nuis", None), P("nuis", None))
    return jax.shard_map(body, mesh=mesh, in_specs=in_specs, out_specs=out_specs, check_vma=False)
```

```python
import jax
import jax.numpy as jnp
from jax import lax
from jax.experimental import pallas as pl
from jax.experimental.pallas import tpu as pltpu
from jax.sharding import PartitionSpec as P

MESH = pl.DeviceIdType.MESH
F32, BF16 = jnp.float32, jnp.bfloat16
HIGHEST = lax.Precision.HIGHEST
ROWS, COLS, SHARE, PEERS = 1536, 256, 48, 32
HALF = ROWS // 2
PIV = 32


def dot0(a, b, precision=None):
    return lax.dot_general(
        a, b, (((0,), (0,)), ((), ())), preferred_element_type=F32, precision=precision
    )


def split2(v):
    hi = v.astype(BF16).astype(F32)
    return hi, (v - hi).astype(BF16).astype(F32)


def split3(v):
    hi, mid = split2(v)
    return hi, mid, (v - hi) - mid


def lane_of(rows, lanes=128):
    return lax.broadcasted_iota(jnp.int32, (rows, lanes), 1)


def invert(block):
    lane = lax.broadcasted_iota(jnp.int32, (PIV, PIV), 1)
    sub = lax.broadcasted_iota(jnp.int32, (PIV, PIV), 0)
    top = lax.broadcasted_iota(jnp.int32, (1, PIV), 1)
    for j in range(PIV):
        inv = 1.0 / block[j : j + 1, j : j + 1]
        row = jnp.where(top == j, inv, block[j : j + 1, :] * inv)
        rest = jnp.where(lane == j, 0.0, block)
        block = jnp.where(sub == j, row, rest - block[:, j : j + 1] * row)
    return block


def rows3(v):
    hi, mid, low = split3(v)
    r = lax.broadcasted_iota(jnp.int32, (8, v.shape[1]), 0)
    out = jnp.where(r == 0, hi, jnp.where(r == 1, mid, jnp.where(r == 2, low, 0.0)))
    return out.astype(BF16)


def kernel(
    lk, mask, nom, obs, pul, rhs, proc, chan, rate, eff,
    grad_o, part_o, imp_o, res_o,
    krow, kcol, wcol, sb, rb, fb, ycol, vh, gt, g3, egs, egr, c3, im, ab,
    pb, precv, osend, orecv,
    a_s, a_r, b_s, b_r, k_s, k_r, q_s, q_r, x_s, x_r, e_s, e_r, o_s, o_r,
):
    n = lax.axis_index("nuis")
    b = lax.axis_index("bins")
    x, y, zh = n // 8, (n // 2) % 4, n % 2
    zl, core = b // 2, b % 2

    def dev(dx=0, dy=0, dz=0):
        return {"nuis": ((x + dx) % 4) * 8 + ((y + dy) % 4) * 2 + (zh + dz) % 2, "bins": b}

    def place(dy=0, dz=0):
        return ((y + dy) % 4) * 2 + (zh + dz) % 2

    def remote(src, dst, s, r, to):
        return pltpu.make_async_remote_copy(
            src_ref=src, dst_ref=dst, send_sem=s, recv_sem=r, device_id=to, device_id_type=MESH
        )

    own = place()
    core_mate = {"nuis": n, "bins": zl * 2 + (1 - core)}
    z_mate = {"nuis": n, "bins": (1 - zl) * 2 + core}

    steps = (0, 1, 3, 2)

    def tile_x(p):
        return (x + steps[p]) % 4

    def keeps(p):
        return tile_x(p) // 2 == core

    def out_dev(p):
        return {"nuis": tile_x(p) * 8 + y * 2 + zh, "bins": x}

    def out_is_self(p):
        return jnp.logical_and(tile_x(p) == x, x == b)

    def in_dev(s):
        return {"nuis": b * 8 + y * 2 + zh, "bins": 2 * s + x // 2}

    def in_is_self(s):
        return jnp.logical_and(b == x, 2 * s + x // 2 == b)

    bar = pltpu.get_barrier_semaphore()

    def greet(k, carry):
        pl.semaphore_signal(
            bar, inc=1, device_id={"nuis": (n + k) % PEERS, "bins": b}, device_id_type=MESH
        )
        return carry

    lax.fori_loop(1, PEERS, greet, 0)
    for mate in (core_mate, z_mate):
        pl.semaphore_signal(bar, inc=1, device_id=mate, device_id_type=MESH)
    expected = jnp.int32(PEERS - 1 + 2)
    others = [(out_dev(p), jnp.logical_and(keeps(p), jnp.logical_not(out_is_self(p)))) for p in range(4)]
    others += [(in_dev(s), jnp.logical_not(in_is_self(s))) for s in range(2)]
    for other, wanted in others:

        @pl.when(wanted)
        def _():
            pl.semaphore_signal(bar, inc=1, device_id=other, device_id_type=MESH)

        expected = expected + jnp.where(wanted, 1, 0)

    rhs_v = rhs[...]
    r_hi, r_mid = split2(rhs_v)
    r_hi, r_mid = r_hi.astype(BF16), r_mid.astype(BF16)
    pulls = rows3(pul[...])
    egs[0, 96:112, :] = jnp.zeros((16, 128), F32)

    def own_rows(i, carry):
        at = pl.ds(pl.multiple_of(i * 128, 128), 128)
        kb = lk[at, :] * mask[pl.ds(i, 1), :].astype(F32).astype(BF16)
        krow[own, at, :] = kb
        kcol[x, at, :] = kb
        e = lax.dot_general(pulls, kb, (((1,), (1,)), ((), ())), preferred_element_type=F32)
        egs[0, pl.ds(96 + i, 1), :] = e[0:1] + e[1:2] + e[2:3]
        m = jnp.dot(kb, r_hi, preferred_element_type=F32) + jnp.dot(
            kb, r_mid, preferred_element_type=F32
        )
        sb[at, :] = m.astype(BF16)
        return carry

    lax.fori_loop(0, 12, own_rows, 0)

    gram = dot0(rhs_v, rhs_v, HIGHEST)
    for i, part in enumerate((gram[0:128, 0:128], gram[128:256, 0:128], gram[128:256, 128:256])):
        gt[128 * i : 128 * (i + 1), :] = part
    quarter = pl.ds(pl.multiple_of(b * 96, 8), 96)
    egs[0, 0:96, :] = gt[quarter, :]

    pl.semaphore_wait(bar, expected)

    def eg_copy(stage, d):
        to = dev(dx=d) if stage == 0 else dev(dy=d) if stage == 1 else dev(dz=d)
        slot = 3 * stage + d - 1
        return remote(egs.at[stage], egr.at[slot], q_s.at[slot], q_r.at[slot], to)

    def eg_peers(stage):
        return range(1, 2 if stage == 2 else 4)

    def eg_start(stage):
        for d in eg_peers(stage):
            eg_copy(stage, d).start()

    def eg_sum(stage):
        total = egs[stage]
        for d in eg_peers(stage):
            eg_copy(stage, d).wait_recv()
            total = total + egr[3 * stage + d - 1]
        return total

    eg_start(0)

    def sum_copy(k):
        to = (n + k) % PEERS
        return remote(
            sb.at[pl.ds(pl.multiple_of(to * SHARE, 16), SHARE)], rb.at[k], a_s.at[k], a_r.at[k],
            {"nuis": to, "bins": b},
        )

    def start_sum(k, carry):
        sum_copy(k).start()
        return carry

    lax.fori_loop(1, PEERS, start_sum, 0)

    def row_copy(i, slot, to, lo=0, size=ROWS):
        ref = krow.at[slot, pl.ds(lo, size)]
        return remote(ref, ref, k_s.at[i], k_r.at[i], to)

    def col_copy(i, slot, to, lo=0, size=ROWS):
        ref = kcol.at[slot, pl.ds(lo, size)]
        return remote(ref, ref, k_s.at[i], k_r.at[i], to)

    up_x, down_x = (x + 1) % 4, (x + 3) % 4
    far_x = (x + 2) % 4
    copies = {
        0: (lambda: row_copy(0, own, dev(dy=1)), lambda: row_copy(0, place(3), dev(dy=3))),
        1: (lambda: row_copy(1, own, dev(dy=3)), lambda: row_copy(1, place(1), dev(dy=1))),
        2: (lambda: row_copy(2, own, dev(dz=1)), lambda: row_copy(2, place(0, 1), dev(dz=1))),
        3: (lambda: col_copy(3, x, dev(dx=1)), lambda: col_copy(3, down_x, dev(dx=3))),
        4: (lambda: col_copy(4, x, dev(dx=3)), lambda: col_copy(4, up_x, dev(dx=1))),
        5: (lambda: row_copy(5, place(3), dev(dy=1), 0, HALF),
            lambda: row_copy(5, place(2), dev(dy=3), 0, HALF)),
        6: (lambda: row_copy(6, place(1), dev(dy=3), HALF, HALF),
            lambda: row_copy(6, place(2), dev(dy=1), HALF, HALF)),
        7: (lambda: row_copy(7, place(0, 1), dev(dy=1)),
            lambda: row_copy(7, place(3, 1), dev(dy=3))),
        8: (lambda: row_copy(8, place(0, 1), dev(dy=3)),
            lambda: row_copy(8, place(1, 1), dev(dy=1))),
        9: (lambda: row_copy(9, place(3, 1), dev(dy=1), 0, HALF),
            lambda: row_copy(9, place(2, 1), dev(dy=3), 0, HALF)),
        10: (lambda: row_copy(10, place(1, 1), dev(dy=3), HALF, HALF),
             lambda: row_copy(10, place(2, 1), dev(dy=1), HALF, HALF)),
        11: (lambda: col_copy(11, down_x, dev(dx=1), 0, HALF),
             lambda: col_copy(11, far_x, dev(dx=3), 0, HALF)),
        12: (lambda: col_copy(12, up_x, dev(dx=3), HALF, HALF),
             lambda: col_copy(12, far_x, dev(dx=1), HALF, HALF)),
    }

    def send(*which):
        for i in which:
            copies[i][0]().start()

    def arrive(*which):
        for i in which:
            copies[i][1]().wait_recv()

    send(0, 1, 2, 3, 4)

    egs[1] = eg_sum(0)
    eg_start(1)

    def wait_sum(k, acc):
        sum_copy(k).wait_recv()
        return acc + rb[k].astype(F32)

    mine = pl.ds(pl.multiple_of(n * SHARE, 16), SHARE)
    fb[mine, :] = lax.fori_loop(1, PEERS, wait_sum, sb[mine, :].astype(F32)).astype(BF16)

    def share_copy(k):
        return remote(
            fb.at[mine], fb.at[mine], b_s.at[k], b_r.at[k],
            {"nuis": (n + k) % PEERS, "bins": b},
        )

    def share_arrival(k):
        origin = (n + PEERS - k) % PEERS
        ref = fb.at[pl.ds(pl.multiple_of(origin * SHARE, 16), SHARE)]
        return remote(ref, ref, b_s.at[k], b_r.at[k], {"nuis": origin, "bins": b})

    def start_share(k, carry):
        share_copy(k).start()
        return carry

    lax.fori_loop(1, PEERS, start_share, 0)

    egs[2] = eg_sum(1)
    eg_start(2)

    arrive(0)
    send(5)
    arrive(1)
    send(6)
    arrive(2)
    send(7, 8)
    arrive(3)
    send(11)
    arrive(4)
    send(12)

    egs[3] = eg_sum(2)
    g3[quarter, :] = egs[3, 0:96, :]

    def yields_of(i, acc):
        at = pl.ds(pl.multiple_of(i * 128, 128), 128)
        scale = rate[proc[i]] * eff[chan[i]]
        yl = nom[pl.ds(i, 1), :] * scale * jnp.exp(egs[3, pl.ds(96 + i, 1), :])
        ycol[at, :] = jnp.transpose(jnp.broadcast_to(yl, (128, 128)))
        return acc + jnp.dot(
            rows3(yl - obs[pl.ds(i, 1), :]), krow[own, at, :], preferred_element_type=F32
        )

    slope = lax.fori_loop(0, 12, yields_of, jnp.zeros((8, COLS), F32))
    im[0, 256:264, :] = jnp.broadcast_to(slope[0:1] + slope[1:2] + slope[2:3], (8, COLS))

    def weigh(tiles):
        def step(i, carry):
            at = pl.ds(pl.multiple_of(i * 128, 128), 128)
            yl = ycol[at, :]
            yl = jnp.concatenate([yl, yl], axis=1)
            for p in tiles:
                kc = kcol[tile_x(p), at, :].astype(F32)
                wcol[at, 256 * p : 256 * (p + 1)] = (yl * kc).astype(BF16)
            return carry

        lax.fori_loop(0, 12, step, 0)

    weigh((0, 1, 2))

    def wait_share(k, carry):
        share_arrival(k).wait_recv()
        return carry

    lax.fori_loop(1, PEERS, wait_share, 0)

    def all_rows(i, carry):
        at = pl.ds(pl.multiple_of(i * 128, 128), 128)
        yl = ycol[at, :]
        vh[at, :] = (jnp.concatenate([yl, yl], axis=1) * fb[at, :].astype(F32)).astype(BF16)
        return carry

    lax.fori_loop(0, 12, all_rows, 0)
    left = dot0(fb[...], vh[:, 0:128])
    c3[0, 0:256, :] = left
    c3[0, 256:384, :] = dot0(fb[:, 128:256], vh[:, 128:256])
    c_core = remote(c3.at[0], c3.at[1], x_s.at[0], x_r.at[0], core_mate)
    c_core.start()
    g_core = remote(g3.at[quarter], g3.at[quarter], x_s.at[4], x_r.at[4], core_mate)
    g_core.start()
    im[0, 0:256, :] = dot0(wcol[:, 0:256], fb[...])
    i_core = remote(im.at[0], im.at[1], x_s.at[1], x_r.at[1], core_mate)
    i_core.start()
    mate_quarter = pl.ds(pl.multiple_of((zl * 2 + 1 - core) * 96, 8), 96)
    g_core_in = remote(g3.at[mate_quarter], g3.at[mate_quarter], x_s.at[4], x_r.at[4], core_mate)
    both = pl.ds(pl.multiple_of(zl * 192, 8), 192)
    other = pl.ds(pl.multiple_of((1 - zl) * 192, 8), 192)
    g_z = remote(g3.at[both], g3.at[both], x_s.at[5], x_r.at[5], z_mate)
    g_z_in = remote(g3.at[other], g3.at[other], x_s.at[5], x_r.at[5], z_mate)
    c_z = remote(c3.at[2], c3.at[3], x_s.at[2], x_r.at[2], z_mate)
    i_z = remote(im.at[2], im.at[3], x_s.at[3], x_r.at[3], z_mate)

    def slot_of(k):
        j = k % 4
        return place(j + j // 2 - 2 * (j // 3), k // 4)

    def half_copy(k, p):
        return remote(pb.at[k, p], precv.at[k, p], e_s.at[k, p], e_r.at[k, p], core_mate)

    def multiply(k, tiles):
        first, count = tiles[0], len(tiles)
        part = dot0(krow[slot_of(k)], wcol[:, 256 * first : 256 * (first + count)])
        for i, p in enumerate(tiles):
            pb[k, p] = part[:, 256 * i : 256 * (i + 1)]

            @pl.when(jnp.logical_not(keeps(p)))
            def _():
                half_copy(k, p).start()

    def out_copy(k, p):
        return remote(
            osend.at[k, p], orecv.at[zl, slot_of(k)], o_s.at[k, p], o_r.at[zl, k], out_dev(p)
        )

    def own_copy(k, p):
        return pltpu.make_async_copy(osend.at[k, p], orecv.at[zl, slot_of(k)], o_r.at[zl, k])

    def hand_out(k, tiles):
        for p in tiles:

            @pl.when(keeps(p))
            def _():
                half_copy(k, p).wait_recv()
                osend[k, p] = (pb[k, p] + precv[k, p]).astype(BF16)

                @pl.when(out_is_self(p))
                def _():
                    own_copy(k, p).start()

                @pl.when(jnp.logical_not(out_is_self(p)))
                def _():
                    out_copy(k, p).start()

    def each(act, blocks, tiles):
        lo, hi = blocks

        def step(k, carry):
            act(k, tiles)
            return carry

        lax.fori_loop(lo, hi, step, 0)

    near, far, every = (0, 1, 2), (3,), (0, 1, 2, 3)
    each(multiply, (0, 3), near)
    each(multiply, (4, 5), near)

    c_core.wait_recv()
    c3[2] = c3[0] + c3[1]
    c_z.start()
    g_core_in.wait_recv()
    g_z.start()
    i_core.wait_recv()
    im[2] = im[0] + im[1]
    i_z.start()

    each(hand_out, (0, 3), near)
    each(hand_out, (4, 5), near)

    arrive(11, 12)
    weigh(far)
    each(multiply, (0, 3), far)
    each(multiply, (4, 5), far)
    each(hand_out, (0, 3), far)
    each(hand_out, (4, 5), far)

    arrive(5, 6)
    each(multiply, (3, 4), every)
    arrive(7)
    send(9)
    arrive(8)
    send(10)
    each(hand_out, (3, 4), every)
    each(multiply, (5, 7), every)
    each(hand_out, (5, 7), every)
    arrive(9, 10)
    each(multiply, (7, 8), every)
    each(hand_out, (7, 8), every)

    g_z_in.wait_recv()
    c_z.wait_recv()
    total = c3[2] + c3[3] + g3[...]
    for start, blocks in ((0, total), (256, g3[...])):
        ab[0:128, start : start + 128] = blocks[0:128]
        ab[128:256, start : start + 128] = blocks[128:256]
        ab[0:128, start + 128 : start + 256] = jnp.transpose(blocks[128:256])
        ab[128:256, start + 128 : start + 256] = blocks[256:384]

    def eliminate(i, carry):
        pivot = invert(ab[0:PIV, 0:PIV])
        head = jnp.dot(pivot, ab[0:PIV, :], preferred_element_type=F32, precision=HIGHEST)
        rest = ab[PIV:256, :] - jnp.dot(
            ab[PIV:256, 0:PIV], head, preferred_element_type=F32, precision=HIGHEST
        )
        ab[0 : 256 - PIV, 0:256] = pltpu.roll(rest[:, 0:256], 256 - PIV, 1)
        ab[0 : 256 - PIV, 256:512] = rest[:, 256:512]
        ab[256 - PIV : 256, 0:256] = pltpu.roll(head[:, 0:256], 256 - PIV, 1)
        ab[256 - PIV : 256, 256:512] = head[:, 256:512]
        return carry

    lax.fori_loop(0, 256 // PIV, eliminate, 0)
    step = ab[:, 256:512]
    imp_o[...] = jnp.dot(rhs_v, step, preferred_element_type=F32, precision=HIGHEST)
    i_z.wait_recv()
    image = rhs_v + (im[2, 0:256, :] + im[3, 0:256, :])
    res_o[...] = rhs_v - jnp.dot(image, step, preferred_element_type=F32, precision=HIGHEST)
    grad_o[...] = im[2, 256:257, :] + im[3, 256:257, :] + pul[...]

    def finish(k, carry):
        q = slot_of(k)
        for s in range(2):
            pltpu.make_async_copy(orecv.at[s, q], orecv.at[s, q], o_r.at[s, k]).wait()
        part_o[q] = orecv[0, q].astype(F32) + orecv[1, q].astype(F32)
        return carry

    lax.fori_loop(0, 8, finish, 0)

    def drain_small(k, carry):
        sum_copy(k).wait_send()
        share_copy(k).wait_send()
        return carry

    lax.fori_loop(1, PEERS, drain_small, 0)
    for stage in range(3):
        for d in eg_peers(stage):
            eg_copy(stage, d).wait_send()
    for i in range(13):
        copies[i][0]().wait_send()
    for copy in (c_core, c_z, i_core, i_z, g_core, g_z):
        copy.wait_send()

    def drain_blocks(k, carry):
        for p in range(4):

            @pl.when(jnp.logical_not(keeps(p)))
            def _():
                half_copy(k, p).wait_send()

            @pl.when(jnp.logical_and(keeps(p), jnp.logical_not(out_is_self(p))))
            def _():
                out_copy(k, p).wait_send()

        return carry

    lax.fori_loop(0, 8, drain_blocks, 0)


def body(
    log_kappa, block_mask, process, channel, nominal, observed, process_rate, efficiency,
    nuisance_pulls, impact_rhs,
):
    vmem = pl.BlockSpec(memory_space=pltpu.VMEM)
    smem = pl.BlockSpec(memory_space=pltpu.SMEM)
    dma = pltpu.SemaphoreType.DMA
    gradient, parts, impacts, residual = pl.pallas_call(
        kernel,
        name="gauss_newton",
        out_shape=(
            jax.ShapeDtypeStruct((1, COLS), F32),
            jax.ShapeDtypeStruct((8, 256, COLS), F32),
            jax.ShapeDtypeStruct((256, 256), F32),
            jax.ShapeDtypeStruct((256, 256), F32),
        ),
        in_specs=[vmem] * 6 + [smem] * 4,
        out_specs=(vmem,) * 4,
        scratch_shapes=[
            pltpu.VMEM((8, ROWS, COLS), BF16),
            pltpu.VMEM((4, ROWS, COLS), BF16),
            pltpu.VMEM((ROWS, 1024), BF16),
            pltpu.VMEM((ROWS, COLS), BF16),
            pltpu.VMEM((PEERS, SHARE, COLS), BF16),
            pltpu.VMEM((ROWS, COLS), BF16),
            pltpu.VMEM((ROWS, 128), F32),
            pltpu.VMEM((ROWS, COLS), BF16),
            pltpu.VMEM((384, 128), F32),
            pltpu.VMEM((384, 128), F32),
            pltpu.VMEM((4, 112, 128), F32),
            pltpu.VMEM((7, 112, 128), F32),
            pltpu.VMEM((4, 384, 128), F32),
            pltpu.VMEM((4, 264, COLS), F32),
            pltpu.VMEM((256, 512), F32),
            pltpu.VMEM((8, 4, 256, 256), F32),
            pltpu.VMEM((8, 4, 256, 256), F32),
            pltpu.VMEM((8, 4, 256, 256), BF16),
            pltpu.VMEM((2, 8, 256, 256), BF16),
            dma((PEERS,)), dma((PEERS,)), dma((PEERS,)), dma((PEERS,)),
            dma((13,)), dma((13,)), dma((7,)), dma((7,)), dma((6,)), dma((6,)),
            dma((8, 4)), dma((8, 4)), dma((8, 4)), dma((2, 8)),
        ],
        compiler_params=pltpu.CompilerParams(
            collective_id=0, has_side_effects=True, vmem_limit_bytes=62 * 2**20
        ),
    )(
        log_kappa, block_mask, nominal.reshape(12, 128), observed.reshape(12, 128),
        nuisance_pulls.reshape(1, COLS), impact_rhs, process, channel, process_rate, efficiency,
    )
    tile_rows = 8 * 256
    row = lax.axis_index("bins") * tile_rows + lax.broadcasted_iota(jnp.int32, (tile_rows, COLS), 0)
    col = lax.axis_index("nuis") * COLS + lax.broadcasted_iota(jnp.int32, (tile_rows, COLS), 1)
    hessian = parts.reshape(tile_rows, COLS) + (row == col).astype(F32)
    return gradient.reshape(COLS), hessian, impacts, residual


def solution(mesh):
    in_specs = (
        P("bins", "nuis"),
        P("bins", "nuis"),
        P("bins"),
        P("bins"),
        P("bins"),
        P("bins"),
        P(),
        P(),
        P("nuis"),
        P("nuis", None),
    )
    out_specs = (P("nuis"), P("bins", "nuis"), P("nuis", None), P("nuis", None))
    return jax.shard_map(body, mesh=mesh, in_specs=in_specs, out_specs=out_specs, check_vma=False)
```

```python
import jax
import jax.numpy as jnp
from jax import lax
from jax.experimental import pallas as pl
from jax.experimental.pallas import tpu as pltpu
from jax.sharding import PartitionSpec as P

MESH = pl.DeviceIdType.MESH
F32, BF16 = jnp.float32, jnp.bfloat16
HIGHEST = lax.Precision.HIGHEST
ROWS, COLS, SHARE, PLANE = 1536, 256, 48, 8
HALF = ROWS // 2
FIRST = 1024
LINE = ROWS // 4
PIV, PANEL = 64, 8


def dot0(a, b, precision=None):
    return lax.dot_general(
        a, b, (((0,), (0,)), ((), ())), preferred_element_type=F32, precision=precision
    )


def split2(v):
    hi = v.astype(BF16).astype(F32)
    return hi, (v - hi).astype(BF16).astype(F32)


def split3(v):
    hi, mid = split2(v)
    return hi, mid, (v - hi) - mid


def lane_of(rows, lanes=128):
    return lax.broadcasted_iota(jnp.int32, (rows, lanes), 1)


def invert(block):
    lane = lax.broadcasted_iota(jnp.int32, (PIV, PIV), 1)
    sub = lax.broadcasted_iota(jnp.int32, (PIV, PIV), 0)
    wide = lax.broadcasted_iota(jnp.int32, (PIV, 128), 0)
    for first in range(0, PIV, PANEL):
        cols = [
            jnp.broadcast_to(block[:, first + k : first + k + 1], (PIV, 128)) for k in range(PANEL)
        ]
        used = []
        for j in range(PANEL):
            at, col = first + j, cols[j]
            inv = 1.0 / col[at : at + 1, :]
            used.append((col, inv))
            for k in range(PANEL):
                if k != j:
                    row = cols[k][at : at + 1, :] * inv
                    cols[k] = jnp.where(wide == at, row, cols[k] - col * row)
            cols[j] = jnp.where(wide == at, inv, -col * inv)
        for j in range(PANEL):
            at, (col, inv) = first + j, used[j]
            row = block[at : at + 1, :] * inv[:, 0:PIV]
            block = jnp.where(sub == at, row, block - col[:, 0:PIV] * row)
        for k in range(PANEL):
            block = jnp.where(lane == first + k, cols[k][:, 0:PIV], block)
    return block


def rows3(v):
    hi, mid, low = split3(v)
    r = lax.broadcasted_iota(jnp.int32, (8, v.shape[1]), 0)
    out = jnp.where(r == 0, hi, jnp.where(r == 1, mid, jnp.where(r == 2, low, 0.0)))
    return out.astype(BF16)


def kernel(
    lk, mask, nom, obs, pul, rhs, proc, chan, rate, eff,
    grad_o, part_o, imp_o, res_o,
    krow, kcol, wcol, sb, xr, m1, pr, fb, ycol, vh, gt, g4, egs, egx, eps, epr, c3, im, ab,
    pb, precv, osend, orecv,
    a_s, a_r, p_s, p_r, b_s, b_r, k_s, k_r, x_s, x_r, e_s, e_r, o_s, o_r,
):
    n = lax.axis_index("nuis")
    b = lax.axis_index("bins")
    x, y, zh = n // 8, (n // 2) % 4, n % 2
    zl, core = b // 2, b % 2

    def dev(dx=0, dy=0, dz=0):
        return {"nuis": ((x + dx) % 4) * 8 + ((y + dy) % 4) * 2 + (zh + dz) % 2, "bins": b}

    def place(dy=0, dz=0):
        return ((y + dy) % 4) * 2 + (zh + dz) % 2

    def remote(src, dst, s, r, to):
        return pltpu.make_async_remote_copy(
            src_ref=src, dst_ref=dst, send_sem=s, recv_sem=r, device_id=to, device_id_type=MESH
        )

    own = place()

    def line_dev(d):
        return {"nuis": ((x + d) % 4) * PLANE + own, "bins": b}

    def plane_dev(d):
        return {"nuis": x * PLANE + (own + d) % PLANE, "bins": b}

    core_mate = {"nuis": n, "bins": zl * 2 + (1 - core)}
    z_mate = {"nuis": n, "bins": (1 - zl) * 2 + core}

    steps = (0, 1, 3, 2)

    def tile_x(p):
        return (x + steps[p]) % 4

    def keeps(p):
        return tile_x(p) // 2 == core

    def out_dev(p):
        return {"nuis": tile_x(p) * 8 + y * 2 + zh, "bins": x}

    def out_is_self(p):
        return jnp.logical_and(tile_x(p) == x, x == b)

    def in_dev(s):
        return {"nuis": b * 8 + y * 2 + zh, "bins": 2 * s + x // 2}

    def in_is_self(s):
        return jnp.logical_and(b == x, 2 * s + x // 2 == b)

    bar = pltpu.get_barrier_semaphore()

    def greet_line(d, carry):
        pl.semaphore_signal(bar, inc=1, device_id=line_dev(d), device_id_type=MESH)
        return carry

    def greet_plane(d, carry):
        pl.semaphore_signal(bar, inc=1, device_id=plane_dev(d), device_id_type=MESH)
        return carry

    lax.fori_loop(1, 4, greet_line, 0)
    lax.fori_loop(1, PLANE, greet_plane, 0)
    for mate in (core_mate, z_mate):
        pl.semaphore_signal(bar, inc=1, device_id=mate, device_id_type=MESH)
    expected = jnp.int32(3 + PLANE - 1 + 2)
    others = [(out_dev(p), jnp.logical_and(keeps(p), jnp.logical_not(out_is_self(p)))) for p in range(4)]
    others += [(in_dev(s), jnp.logical_not(in_is_self(s))) for s in range(2)]
    for other, wanted in others:

        @pl.when(wanted)
        def _():
            pl.semaphore_signal(bar, inc=1, device_id=other, device_id_type=MESH)

        expected = expected + jnp.where(wanted, 1, 0)

    rhs_v = rhs[...]
    r_hi, r_mid = split2(rhs_v)
    r_hi, r_mid = r_hi.astype(BF16), r_mid.astype(BF16)
    pulls = rows3(pul[...])
    egs[0, 128:144, :] = jnp.zeros((16, 128), F32)

    def own_rows(i, carry):
        at = pl.ds(pl.multiple_of(i * 128, 128), 128)
        kb = lk[at, :] * mask[pl.ds(i, 1), :].astype(F32).astype(BF16)
        krow[own, at, :] = kb
        kcol[x, at, :] = kb
        e = lax.dot_general(pulls, kb, (((1,), (1,)), ((), ())), preferred_element_type=F32)
        egs[0, pl.ds(128 + i, 1), :] = e[0:1] + e[1:2] + e[2:3]
        m = jnp.dot(kb, r_hi, preferred_element_type=F32) + jnp.dot(
            kb, r_mid, preferred_element_type=F32
        )
        sb[at, :] = m.astype(BF16)
        return carry

    lax.fori_loop(0, 12, own_rows, 0)

    gram = dot0(rhs_v, rhs_v, HIGHEST)
    gt[0:256, :] = gram[:, 0:128]
    gt[256:512, :] = gram[:, 128:256]
    egs[0, 0:128, :] = gt[pl.ds(pl.multiple_of(b * 128, 128), 128), :]

    pl.semaphore_wait(bar, expected)

    def line_rows(at):
        return pl.ds(pl.multiple_of(at * LINE, 16), LINE)

    def m_line(d):
        return remote(
            sb.at[line_rows((x + d) % 4)], xr.at[d - 1], a_s.at[d], a_r.at[d], line_dev(d)
        )

    def eg_line(d):
        return remote(egs.at[0], egx.at[d - 1], a_s.at[3 + d], a_r.at[3 + d], line_dev(d))

    for d in range(1, 4):
        eg_line(d).start()
    for d in range(1, 4):
        m_line(d).start()

    def row_copy(i, slot, to, lo=0, size=ROWS):
        ref = krow.at[slot, pl.ds(lo, size)]
        return remote(ref, ref, k_s.at[i], k_r.at[i], to)

    def col_copy(i, slot, to, lo=0, size=ROWS):
        ref = kcol.at[slot, pl.ds(lo, size)]
        return remote(ref, ref, k_s.at[i], k_r.at[i], to)

    up_x, down_x = (x + 1) % 4, (x + 3) % 4
    far_x = (x + 2) % 4
    rest = ROWS - FIRST
    copies = {
        0: (lambda: row_copy(0, own, dev(dy=1), 0, FIRST),
            lambda: row_copy(0, place(3), dev(dy=3), 0, FIRST)),
        1: (lambda: row_copy(1, own, dev(dy=3), 0, FIRST),
            lambda: row_copy(1, place(1), dev(dy=1), 0, FIRST)),
        2: (lambda: row_copy(2, own, dev(dz=1), 0, FIRST),
            lambda: row_copy(2, place(0, 1), dev(dz=1), 0, FIRST)),
        3: (lambda: col_copy(3, x, dev(dx=1), 0, HALF),
            lambda: col_copy(3, down_x, dev(dx=3), 0, HALF)),
        4: (lambda: col_copy(4, x, dev(dx=3), 0, HALF),
            lambda: col_copy(4, up_x, dev(dx=1), 0, HALF)),
        13: (lambda: row_copy(13, own, dev(dy=1), FIRST, rest),
             lambda: row_copy(13, place(3), dev(dy=3), FIRST, rest)),
        14: (lambda: row_copy(14, own, dev(dy=3), FIRST, rest),
             lambda: row_copy(14, place(1), dev(dy=1), FIRST, rest)),
        15: (lambda: row_copy(15, own, dev(dz=1), FIRST, rest),
             lambda: row_copy(15, place(0, 1), dev(dz=1), FIRST, rest)),
        16: (lambda: col_copy(16, x, dev(dx=1), HALF, HALF),
             lambda: col_copy(16, down_x, dev(dx=3), HALF, HALF)),
        17: (lambda: col_copy(17, x, dev(dx=3), HALF, HALF),
             lambda: col_copy(17, up_x, dev(dx=1), HALF, HALF)),
        5: (lambda: row_copy(5, place(3), dev(dy=1), 0, HALF),
            lambda: row_copy(5, place(2), dev(dy=3), 0, HALF)),
        6: (lambda: row_copy(6, place(1), dev(dy=3), HALF, HALF),
            lambda: row_copy(6, place(2), dev(dy=1), HALF, HALF)),
        7: (lambda: row_copy(7, place(0, 1), dev(dy=1), 0, FIRST),
            lambda: row_copy(7, place(3, 1), dev(dy=3), 0, FIRST)),
        8: (lambda: row_copy(8, place(0, 1), dev(dy=3), 0, FIRST),
            lambda: row_copy(8, place(1, 1), dev(dy=1), 0, FIRST)),
        18: (lambda: row_copy(18, place(0, 1), dev(dy=1), FIRST, rest),
             lambda: row_copy(18, place(3, 1), dev(dy=3), FIRST, rest)),
        19: (lambda: row_copy(19, place(0, 1), dev(dy=3), FIRST, rest),
             lambda: row_copy(19, place(1, 1), dev(dy=1), FIRST, rest)),
        9: (lambda: row_copy(9, place(3, 1), dev(dy=1), 0, HALF),
            lambda: row_copy(9, place(2, 1), dev(dy=3), 0, HALF)),
        10: (lambda: row_copy(10, place(1, 1), dev(dy=3), HALF, HALF),
             lambda: row_copy(10, place(2, 1), dev(dy=1), HALF, HALF)),
        11: (lambda: col_copy(11, down_x, dev(dx=1), 0, HALF),
             lambda: col_copy(11, far_x, dev(dx=3), 0, HALF)),
        12: (lambda: col_copy(12, up_x, dev(dx=3), HALF, HALF),
             lambda: col_copy(12, far_x, dev(dx=1), HALF, HALF)),
    }

    def send(*which):
        for i in which:
            copies[i][0]().start()

    def arrive(*which):
        for i in which:
            copies[i][1]().wait_recv()

    send(0, 1, 2)

    total = egs[0]
    for d in range(1, 4):
        eg_line(d).wait_recv()
        total = total + egx[d - 1]
    for q in range(PLANE):
        eps[q, 0:16, :] = total[128:144]
        eps[q, 16:32, :] = total[16 * q : 16 * (q + 1)]
    line = line_rows(x)
    total = sb[line, :].astype(F32)
    for d in range(1, 4):
        m_line(d).wait_recv()
        total = total + xr[d - 1].astype(F32)
    m1[...] = total
    send(3, 4)

    def m_plane(d):
        at = pl.ds(pl.multiple_of((own + d) % PLANE * SHARE, 16), SHARE)
        return remote(m1.at[at], pr.at[d], p_s.at[0, d], p_r.at[0, d], plane_dev(d))

    def e_plane(d):
        src = eps.at[(own + d) % PLANE]
        return remote(src, epr.at[d], p_s.at[1, d], p_r.at[1, d], plane_dev(d))

    def start_plane(d, carry):
        e_plane(d).start()
        m_plane(d).start()
        return carry

    lax.fori_loop(1, PLANE, start_plane, 0)

    def sum_e(d, acc):
        e_plane(d).wait_recv()
        return acc + epr[d]

    def sum_m(d, acc):
        m_plane(d).wait_recv()
        return acc + pr[d]

    mine = pl.ds(pl.multiple_of(x * LINE + own * SHARE, 16), SHARE)
    gram_rows = pl.ds(pl.multiple_of(own * 16, 16), 16)
    total = lax.fori_loop(1, PLANE, sum_e, eps[own])
    egs[1, 0:32, :] = total
    g4[b, gram_rows, :] = total[16:32]
    fb[mine, :] = lax.fori_loop(
        1, PLANE, sum_m, m1[pl.ds(pl.multiple_of(own * SHARE, 16), SHARE), :]
    ).astype(BF16)

    def m_share(d):
        return remote(fb.at[mine], fb.at[mine], b_s.at[0, d], b_r.at[0, d], plane_dev(d))

    def g_share(d):
        ref = g4.at[b, gram_rows]
        return remote(ref, ref, b_s.at[1, d], b_r.at[1, d], plane_dev(d))

    def start_share(d, carry):
        m_share(d).start()
        g_share(d).start()
        return carry

    lax.fori_loop(1, PLANE, start_share, 0)
    send(13, 14, 15)
    arrive(0)
    send(5)
    arrive(2)
    send(8, 7)

    def yields_of(i, acc):
        at = pl.ds(pl.multiple_of(i * 128, 128), 128)
        scale = rate[proc[i]] * eff[chan[i]]
        yl = nom[pl.ds(i, 1), :] * scale * jnp.exp(egs[1, pl.ds(i, 1), :])
        ycol[at, :] = jnp.transpose(jnp.broadcast_to(yl, (128, 128)))
        return acc + jnp.dot(
            rows3(yl - obs[pl.ds(i, 1), :]), krow[own, at, :], preferred_element_type=F32
        )

    slope = lax.fori_loop(0, 12, yields_of, jnp.zeros((8, COLS), F32))
    im[0, 256:264, :] = jnp.broadcast_to(slope[0:1] + slope[1:2] + slope[2:3], (8, COLS))

    def wait_plane(d, carry):
        origin = (own + PLANE - d) % PLANE
        ref = fb.at[pl.ds(pl.multiple_of(x * LINE + origin * SHARE, 16), SHARE)]
        remote(ref, ref, b_s.at[0, d], b_r.at[0, d], plane_dev(d)).wait_recv()
        ref = g4.at[b, pl.ds(pl.multiple_of(origin * 16, 16), 16)]
        remote(ref, ref, b_s.at[1, d], b_r.at[1, d], plane_dev(d)).wait_recv()
        return carry

    lax.fori_loop(1, PLANE, wait_plane, 0)

    def m_all(d, at):
        ref = fb.at[line_rows(at)]
        return remote(ref, ref, a_s.at[6 + d], a_r.at[6 + d], line_dev(d))

    for d in range(1, 4):
        m_all(d, x).start()
    arrive(3)
    send(16, 17, 11)

    def weigh(tiles):
        def step(i, carry):
            at = pl.ds(pl.multiple_of(i * 128, 128), 128)
            yl = ycol[at, :]
            yl = jnp.concatenate([yl, yl], axis=1)
            for p in tiles:
                kc = kcol[tile_x(p), at, :].astype(F32)
                wcol[at, 256 * p : 256 * (p + 1)] = (yl * kc).astype(BF16)
            return carry

        lax.fori_loop(0, 12, step, 0)

    def slot_of(k):
        j = k % 4
        return place(j + j // 2 - 2 * (j // 3), k // 4)

    def half_copy(k, p):
        return remote(pb.at[k, p], precv.at[k, p], e_s.at[k, p], e_r.at[k, p], core_mate)

    def multiply(k, tiles):
        first, count = tiles[0], len(tiles)
        part = dot0(krow[slot_of(k)], wcol[:, 256 * first : 256 * (first + count)])
        for i, p in enumerate(tiles):
            pb[k, p] = part[:, 256 * i : 256 * (i + 1)]

            @pl.when(jnp.logical_not(keeps(p)))
            def _():
                half_copy(k, p).start()

    def out_copy(k, p):
        return remote(
            osend.at[k, p], orecv.at[zl, slot_of(k)], o_s.at[k, p], o_r.at[zl, k], out_dev(p)
        )

    def own_copy(k, p):
        return pltpu.make_async_copy(osend.at[k, p], orecv.at[zl, slot_of(k)], o_r.at[zl, k])

    def hand_out(k, tiles):
        for p in tiles:

            @pl.when(keeps(p))
            def _():
                half_copy(k, p).wait_recv()
                osend[k, p] = (pb[k, p] + precv[k, p]).astype(BF16)

                @pl.when(out_is_self(p))
                def _():
                    own_copy(k, p).start()

                @pl.when(jnp.logical_not(out_is_self(p)))
                def _():
                    out_copy(k, p).start()

    def each(act, blocks, tiles):
        lo, hi = blocks

        def step(k, carry):
            act(k, tiles)
            return carry

        lax.fori_loop(lo, hi, step, 0)

    weigh((0,))
    arrive(1, 13, 14)
    send(6)
    arrive(15)
    send(19, 18)

    diag, near, far, every = (0,), (1, 2), (3,), (0, 1, 2, 3)
    each(multiply, (0, 3), diag)
    each(multiply, (4, 5), diag)
    each(hand_out, (0, 3), diag)
    each(hand_out, (4, 5), diag)


    for d in range(1, 4):
        m_all(d, (x + 4 - d) % 4).wait_recv()

    def all_rows(i, carry):
        at = pl.ds(pl.multiple_of(i * 128, 128), 128)
        yl = ycol[at, :]
        vh[at, :] = (jnp.concatenate([yl, yl], axis=1) * fb[at, :].astype(F32)).astype(BF16)
        return carry

    lax.fori_loop(0, 12, all_rows, 0)
    left = dot0(fb[...], vh[:, 0:128])
    c3[0, 0:256, :] = left
    c3[0, 256:384, :] = dot0(fb[:, 128:256], vh[:, 128:256])
    c_core = remote(c3.at[0], c3.at[1], x_s.at[0], x_r.at[0], core_mate)
    c_core.start()
    g_core = remote(g4.at[b], g4.at[b], x_s.at[4], x_r.at[4], core_mate)
    g_core.start()
    im[0, 0:256, :] = dot0(wcol[:, 0:256], fb[...])
    i_core = remote(im.at[0], im.at[1], x_s.at[1], x_r.at[1], core_mate)
    i_core.start()
    mate = zl * 2 + 1 - core
    g_core_in = remote(g4.at[mate], g4.at[mate], x_s.at[4], x_r.at[4], core_mate)
    both = g4.at[pl.ds(zl * 2, 2)]
    other = g4.at[pl.ds((1 - zl) * 2, 2)]
    g_z = remote(both, both, x_s.at[5], x_r.at[5], z_mate)
    g_z_in = remote(other, other, x_s.at[5], x_r.at[5], z_mate)
    c_z = remote(c3.at[2], c3.at[3], x_s.at[2], x_r.at[2], z_mate)
    i_z = remote(im.at[2], im.at[3], x_s.at[3], x_r.at[3], z_mate)

    c_core.wait_recv()
    c3[2] = c3[0] + c3[1]
    c_z.start()
    g_core_in.wait_recv()
    g_z.start()
    i_core.wait_recv()
    im[2] = im[0] + im[1]
    i_z.start()

    arrive(4, 17)
    send(12)
    arrive(5, 6)
    each(multiply, (3, 4), diag)
    arrive(16)
    weigh((1, 2))
    each(multiply, (0, 5), near)
    each(hand_out, (3, 4), diag)
    each(hand_out, (0, 5), near)
    arrive(7)
    send(9)

    g_z_in.wait_recv()
    c_z.wait_recv()
    total = c3[2] + c3[3]
    ab[0:128, 0:128] = total[0:128] + g4[0]
    ab[128:256, 0:128] = total[128:256] + g4[1]
    ab[0:128, 128:256] = jnp.transpose(total[128:256]) + g4[2]
    ab[128:256, 128:256] = total[256:384] + g4[3]
    for i in range(4):
        row, col = 128 * (i % 2), 256 + 128 * (i // 2)
        ab[row : row + 128, col : col + 128] = g4[i]

    def eliminate(i, carry):
        pivot = invert(ab[0:PIV, 0:PIV])
        head = jnp.dot(pivot, ab[0:PIV, :], preferred_element_type=F32, precision=HIGHEST)
        rest = ab[PIV:256, :] - jnp.dot(
            ab[PIV:256, 0:PIV], head, preferred_element_type=F32, precision=HIGHEST
        )
        ab[0 : 256 - PIV, 0:256] = pltpu.roll(rest[:, 0:256], 256 - PIV, 1)
        ab[0 : 256 - PIV, 256:512] = rest[:, 256:512]
        ab[256 - PIV : 256, 0:256] = pltpu.roll(head[:, 0:256], 256 - PIV, 1)
        ab[256 - PIV : 256, 256:512] = head[:, 256:512]
        return carry

    lax.fori_loop(0, 2, eliminate, 0)
    arrive(8, 19)
    send(10)
    arrive(11, 12)
    weigh(far)
    each(multiply, (0, 5), far)
    each(hand_out, (0, 5), far)
    arrive(18)
    each(multiply, (5, 7), every)
    each(hand_out, (5, 7), every)
    arrive(9, 10)
    each(multiply, (7, 8), every)
    each(hand_out, (7, 8), every)
    lax.fori_loop(2, 4, eliminate, 0)
    step = ab[:, 256:512]
    imp_o[...] = jnp.dot(rhs_v, step, preferred_element_type=F32, precision=HIGHEST)
    i_z.wait_recv()
    image = rhs_v + (im[2, 0:256, :] + im[3, 0:256, :])
    res_o[...] = rhs_v - jnp.dot(image, step, preferred_element_type=F32, precision=HIGHEST)
    grad_o[...] = im[2, 256:257, :] + im[3, 256:257, :] + pul[...]

    def finish(k, carry):
        q = slot_of(k)
        for s in range(2):
            pltpu.make_async_copy(orecv.at[s, q], orecv.at[s, q], o_r.at[s, k]).wait()
        part_o[q] = orecv[0, q].astype(F32) + orecv[1, q].astype(F32)
        return carry

    lax.fori_loop(0, 8, finish, 0)

    for d in range(1, 4):
        eg_line(d).wait_send()
        m_line(d).wait_send()
        m_all(d, x).wait_send()

    def drain_plane(d, carry):
        m_plane(d).wait_send()
        e_plane(d).wait_send()
        m_share(d).wait_send()
        g_share(d).wait_send()
        return carry

    lax.fori_loop(1, PLANE, drain_plane, 0)
    for i in range(20):
        copies[i][0]().wait_send()
    for copy in (c_core, c_z, i_core, i_z, g_core, g_z):
        copy.wait_send()

    def drain_blocks(k, carry):
        for p in range(4):

            @pl.when(jnp.logical_not(keeps(p)))
            def _():
                half_copy(k, p).wait_send()

            @pl.when(jnp.logical_and(keeps(p), jnp.logical_not(out_is_self(p))))
            def _():
                out_copy(k, p).wait_send()

        return carry

    lax.fori_loop(0, 8, drain_blocks, 0)


def body(
    log_kappa, block_mask, process, channel, nominal, observed, process_rate, efficiency,
    nuisance_pulls, impact_rhs,
):
    vmem = pl.BlockSpec(memory_space=pltpu.VMEM)
    smem = pl.BlockSpec(memory_space=pltpu.SMEM)
    dma = pltpu.SemaphoreType.DMA
    gradient, parts, impacts, residual = pl.pallas_call(
        kernel,
        name="gauss_newton",
        out_shape=(
            jax.ShapeDtypeStruct((1, COLS), F32),
            jax.ShapeDtypeStruct((8, 256, COLS), F32),
            jax.ShapeDtypeStruct((256, 256), F32),
            jax.ShapeDtypeStruct((256, 256), F32),
        ),
        in_specs=[vmem] * 6 + [smem] * 4,
        out_specs=(vmem,) * 4,
        scratch_shapes=[
            pltpu.VMEM((8, ROWS, COLS), BF16),
            pltpu.VMEM((4, ROWS, COLS), BF16),
            pltpu.VMEM((ROWS, 1024), BF16),
            pltpu.VMEM((ROWS, COLS), BF16),
            pltpu.VMEM((3, LINE, COLS), BF16),
            pltpu.VMEM((LINE, COLS), F32),
            pltpu.VMEM((PLANE, SHARE, COLS), F32),
            pltpu.VMEM((ROWS, COLS), BF16),
            pltpu.VMEM((ROWS, 128), F32),
            pltpu.VMEM((ROWS, COLS), BF16),
            pltpu.VMEM((512, 128), F32),
            pltpu.VMEM((4, 128, 128), F32),
            pltpu.VMEM((2, 144, 128), F32),
            pltpu.VMEM((3, 144, 128), F32),
            pltpu.VMEM((PLANE, 32, 128), F32),
            pltpu.VMEM((PLANE, 32, 128), F32),
            pltpu.VMEM((4, 384, 128), F32),
            pltpu.VMEM((4, 264, COLS), F32),
            pltpu.VMEM((256, 512), F32),
            pltpu.VMEM((8, 4, 256, 256), F32),
            pltpu.VMEM((8, 4, 256, 256), F32),
            pltpu.VMEM((8, 4, 256, 256), BF16),
            pltpu.VMEM((2, 8, 256, 256), BF16),
            dma((10,)), dma((10,)), dma((2, PLANE)), dma((2, PLANE)), dma((2, PLANE)), dma((2, PLANE)),
            dma((20,)), dma((20,)), dma((6,)), dma((6,)),
            dma((8, 4)), dma((8, 4)), dma((8, 4)), dma((2, 8)),
        ],
        compiler_params=pltpu.CompilerParams(
            collective_id=0, has_side_effects=True, vmem_limit_bytes=62 * 2**20
        ),
    )(
        log_kappa, block_mask, nominal.reshape(12, 128), observed.reshape(12, 128),
        nuisance_pulls.reshape(1, COLS), impact_rhs, process, channel, process_rate, efficiency,
    )
    tile_rows = 8 * 256
    row = lax.axis_index("bins") * tile_rows + lax.broadcasted_iota(jnp.int32, (tile_rows, COLS), 0)
    col = lax.axis_index("nuis") * COLS + lax.broadcasted_iota(jnp.int32, (tile_rows, COLS), 1)
    hessian = parts.reshape(tile_rows, COLS) + (row == col).astype(F32)
    return gradient.reshape(COLS), hessian, impacts, residual


def solution(mesh):
    in_specs = (
        P("bins", "nuis"),
        P("bins", "nuis"),
        P("bins"),
        P("bins"),
        P("bins"),
        P("bins"),
        P(),
        P(),
        P("nuis"),
        P("nuis", None),
    )
    out_specs = (P("nuis"), P("bins", "nuis"), P("nuis", None), P("nuis", None))
    return jax.shard_map(body, mesh=mesh, in_specs=in_specs, out_specs=out_specs, check_vma=False)
```

```python
import jax
import jax.numpy as jnp
from jax import lax
from jax.experimental import pallas as pl
from jax.experimental.pallas import tpu as pltpu
from jax.sharding import PartitionSpec as P

MESH = pl.DeviceIdType.MESH
F32, BF16 = jnp.float32, jnp.bfloat16
HIGHEST = lax.Precision.HIGHEST
ROWS, COLS, SHARE, PLANE = 1536, 256, 48, 8
HALF = ROWS // 2
FIRST = 1280
LINE = ROWS // 4
PIV, PANEL = 64, 8


def dot0(a, b, precision=None):
    return lax.dot_general(
        a, b, (((0,), (0,)), ((), ())), preferred_element_type=F32, precision=precision
    )


def split2(v):
    hi = v.astype(BF16).astype(F32)
    return hi, (v - hi).astype(BF16).astype(F32)


def split3(v):
    hi, mid = split2(v)
    return hi, mid, (v - hi) - mid


def lane_of(rows, lanes=128):
    return lax.broadcasted_iota(jnp.int32, (rows, lanes), 1)


def invert(block):
    lane = lax.broadcasted_iota(jnp.int32, (PIV, PIV), 1)
    sub = lax.broadcasted_iota(jnp.int32, (PIV, PIV), 0)
    wide = lax.broadcasted_iota(jnp.int32, (PIV, 128), 0)
    for first in range(0, PIV, PANEL):
        cols = [
            jnp.broadcast_to(block[:, first + k : first + k + 1], (PIV, 128)) for k in range(PANEL)
        ]
        used = []
        for j in range(PANEL):
            at, col = first + j, cols[j]
            inv = 1.0 / col[at : at + 1, :]
            used.append((col, inv))
            for k in range(PANEL):
                if k != j:
                    row = cols[k][at : at + 1, :] * inv
                    cols[k] = jnp.where(wide == at, row, cols[k] - col * row)
            cols[j] = jnp.where(wide == at, inv, -col * inv)
        for j in range(PANEL):
            at, (col, inv) = first + j, used[j]
            row = block[at : at + 1, :] * inv[:, 0:PIV]
            block = jnp.where(sub == at, row, block - col[:, 0:PIV] * row)
        for k in range(PANEL):
            block = jnp.where(lane == first + k, cols[k][:, 0:PIV], block)
    return block


def rows3(v):
    hi, mid, low = split3(v)
    r = lax.broadcasted_iota(jnp.int32, (8, v.shape[1]), 0)
    out = jnp.where(r == 0, hi, jnp.where(r == 1, mid, jnp.where(r == 2, low, 0.0)))
    return out.astype(BF16)


def kernel(
    lk, mask, nom, obs, pul, rhs, proc, chan, rate, eff,
    grad_o, part_o, imp_o, res_o,
    krow, kcol, wcol, sb, xr, m1, pr, fb, ycol, vh, gt, g4, egs, egx, eps, epr, c3, im, ab,
    pb, precv, osend, ctot, itot, grad_v, imp_v, res_v,
    a_s, a_r, p_s, p_r, b_s, b_r, k_s, k_r, x_s, x_r, w_s, e_s, e_r, o_s, o_r,
):
    n = lax.axis_index("nuis")
    b = lax.axis_index("bins")
    x, y, zh = n // 8, (n // 2) % 4, n % 2
    zl, core = b // 2, b % 2

    def dev(dx=0, dy=0, dz=0):
        return {"nuis": ((x + dx) % 4) * 8 + ((y + dy) % 4) * 2 + (zh + dz) % 2, "bins": b}

    def place(dy=0, dz=0):
        return ((y + dy) % 4) * 2 + (zh + dz) % 2

    def remote(src, dst, s, r, to):
        return pltpu.make_async_remote_copy(
            src_ref=src, dst_ref=dst, send_sem=s, recv_sem=r, device_id=to, device_id_type=MESH
        )

    own = place()
    block = core * 2 + zl

    def line_dev(d):
        return {"nuis": ((x + d) % 4) * PLANE + own, "bins": b}

    def plane_dev(d):
        return {"nuis": x * PLANE + (own + d) % PLANE, "bins": b}

    core_mate = {"nuis": n, "bins": zl * 2 + (1 - core)}
    z_mate = {"nuis": n, "bins": (1 - zl) * 2 + core}

    steps = (0, 1, 3, 2)

    def tile_x(p):
        return (x + steps[p]) % 4

    def keeps(p):
        return tile_x(p) // 2 == core

    def out_dev(p):
        return {"nuis": tile_x(p) * 8 + y * 2 + zh, "bins": x}

    def out_is_self(p):
        return jnp.logical_and(tile_x(p) == x, x == b)

    def in_dev(s):
        return {"nuis": b * 8 + y * 2 + zh, "bins": 2 * s + x // 2}

    def in_is_self(s):
        return jnp.logical_and(b == x, 2 * s + x // 2 == b)

    bar = pltpu.get_barrier_semaphore()

    def greet_line(d, carry):
        pl.semaphore_signal(bar, inc=1, device_id=line_dev(d), device_id_type=MESH)
        return carry

    def greet_plane(d, carry):
        pl.semaphore_signal(bar, inc=1, device_id=plane_dev(d), device_id_type=MESH)
        return carry

    lax.fori_loop(1, 4, greet_line, 0)
    lax.fori_loop(1, PLANE, greet_plane, 0)
    for mate in (core_mate, z_mate):
        pl.semaphore_signal(bar, inc=1, device_id=mate, device_id_type=MESH)
    expected = jnp.int32(3 + PLANE - 1 + 2)
    others = [(out_dev(p), jnp.logical_and(keeps(p), jnp.logical_not(out_is_self(p)))) for p in range(4)]
    others += [(in_dev(s), jnp.logical_not(in_is_self(s))) for s in range(2)]
    for other, wanted in others:

        @pl.when(wanted)
        def _():
            pl.semaphore_signal(bar, inc=1, device_id=other, device_id_type=MESH)

        expected = expected + jnp.where(wanted, 1, 0)

    rhs_v = rhs[...]
    r_hi, r_mid = split2(rhs_v)
    r_hi, r_mid = r_hi.astype(BF16), r_mid.astype(BF16)
    pulls = rows3(pul[...])
    egs[0, 128:144, :] = jnp.zeros((16, 128), F32)

    def own_rows(i, carry):
        at = pl.ds(pl.multiple_of(i * 128, 128), 128)
        kb = lk[at, :] * mask[pl.ds(i, 1), :].astype(F32).astype(BF16)
        krow[own, at, :] = kb
        kcol[x, at, :] = kb
        e = lax.dot_general(pulls, kb, (((1,), (1,)), ((), ())), preferred_element_type=F32)
        egs[0, pl.ds(128 + i, 1), :] = e[0:1] + e[1:2] + e[2:3]
        m = jnp.dot(kb, r_hi, preferred_element_type=F32) + jnp.dot(
            kb, r_mid, preferred_element_type=F32
        )
        sb[at, :] = m.astype(BF16)
        return carry

    lax.fori_loop(0, 12, own_rows, 0)

    gram = dot0(rhs_v, rhs_v, HIGHEST)
    gt[0:256, :] = gram[:, 0:128]
    gt[256:512, :] = gram[:, 128:256]
    egs[0, 0:128, :] = gt[pl.ds(pl.multiple_of(b * 128, 128), 128), :]

    pl.semaphore_wait(bar, expected)

    def line_rows(at):
        return pl.ds(pl.multiple_of(at * LINE, 16), LINE)

    def m_line(d):
        return remote(
            sb.at[line_rows((x + d) % 4)], xr.at[d - 1], a_s.at[d], a_r.at[d], line_dev(d)
        )

    def eg_line(d):
        return remote(egs.at[0], egx.at[d - 1], a_s.at[3 + d], a_r.at[3 + d], line_dev(d))

    for d in range(1, 4):
        eg_line(d).start()
    for d in range(1, 4):
        m_line(d).start()

    def row_copy(i, slot, to, lo=0, size=ROWS):
        ref = krow.at[slot, pl.ds(lo, size)]
        return remote(ref, ref, k_s.at[i], k_r.at[i], to)

    def col_copy(i, slot, to, lo=0, size=ROWS):
        ref = kcol.at[slot, pl.ds(lo, size)]
        return remote(ref, ref, k_s.at[i], k_r.at[i], to)

    up_x, down_x = (x + 1) % 4, (x + 3) % 4
    far_x = (x + 2) % 4
    rest = ROWS - FIRST
    copies = {
        0: (lambda: row_copy(0, own, dev(dy=1), 0, FIRST),
            lambda: row_copy(0, place(3), dev(dy=3), 0, FIRST)),
        1: (lambda: row_copy(1, own, dev(dy=3), 0, FIRST),
            lambda: row_copy(1, place(1), dev(dy=1), 0, FIRST)),
        2: (lambda: row_copy(2, own, dev(dz=1), 0, FIRST),
            lambda: row_copy(2, place(0, 1), dev(dz=1), 0, FIRST)),
        3: (lambda: col_copy(3, x, dev(dx=1), 0, HALF),
            lambda: col_copy(3, down_x, dev(dx=3), 0, HALF)),
        4: (lambda: col_copy(4, x, dev(dx=3), 0, HALF),
            lambda: col_copy(4, up_x, dev(dx=1), 0, HALF)),
        13: (lambda: row_copy(13, own, dev(dy=1), FIRST, rest),
             lambda: row_copy(13, place(3), dev(dy=3), FIRST, rest)),
        14: (lambda: row_copy(14, own, dev(dy=3), FIRST, rest),
             lambda: row_copy(14, place(1), dev(dy=1), FIRST, rest)),
        15: (lambda: row_copy(15, own, dev(dz=1), FIRST, rest),
             lambda: row_copy(15, place(0, 1), dev(dz=1), FIRST, rest)),
        16: (lambda: col_copy(16, x, dev(dx=1), HALF, HALF),
             lambda: col_copy(16, down_x, dev(dx=3), HALF, HALF)),
        17: (lambda: col_copy(17, x, dev(dx=3), HALF, HALF),
             lambda: col_copy(17, up_x, dev(dx=1), HALF, HALF)),
        5: (lambda: row_copy(5, place(3), dev(dy=1), 0, HALF),
            lambda: row_copy(5, place(2), dev(dy=3), 0, HALF)),
        6: (lambda: row_copy(6, place(1), dev(dy=3), HALF, HALF),
            lambda: row_copy(6, place(2), dev(dy=1), HALF, HALF)),
        7: (lambda: row_copy(7, place(0, 1), dev(dy=1), 0, FIRST),
            lambda: row_copy(7, place(3, 1), dev(dy=3), 0, FIRST)),
        8: (lambda: row_copy(8, place(0, 1), dev(dy=3), 0, FIRST),
            lambda: row_copy(8, place(1, 1), dev(dy=1), 0, FIRST)),
        18: (lambda: row_copy(18, place(0, 1), dev(dy=1), FIRST, rest),
             lambda: row_copy(18, place(3, 1), dev(dy=3), FIRST, rest)),
        19: (lambda: row_copy(19, place(0, 1), dev(dy=3), FIRST, rest),
             lambda: row_copy(19, place(1, 1), dev(dy=1), FIRST, rest)),
        9: (lambda: row_copy(9, place(3, 1), dev(dy=1), 0, HALF),
            lambda: row_copy(9, place(2, 1), dev(dy=3), 0, HALF)),
        10: (lambda: row_copy(10, place(1, 1), dev(dy=3), HALF, HALF),
             lambda: row_copy(10, place(2, 1), dev(dy=1), HALF, HALF)),
        11: (lambda: col_copy(11, down_x, dev(dx=1), 0, HALF),
             lambda: col_copy(11, far_x, dev(dx=3), 0, HALF)),
        12: (lambda: col_copy(12, up_x, dev(dx=3), HALF, HALF),
             lambda: col_copy(12, far_x, dev(dx=1), HALF, HALF)),
    }

    def send(*which):
        for i in which:
            copies[i][0]().start()

    def arrive(*which):
        for i in which:
            copies[i][1]().wait_recv()

    send(0, 1, 2)

    total = egs[0]
    for d in range(1, 4):
        eg_line(d).wait_recv()
        total = total + egx[d - 1]
    for q in range(PLANE):
        eps[q, 0:16, :] = total[128:144]
        eps[q, 16:32, :] = total[16 * q : 16 * (q + 1)]
    line = line_rows(x)
    total = sb[line, :].astype(F32)
    for d in range(1, 4):
        m_line(d).wait_recv()
        total = total + xr[d - 1].astype(F32)
    m1[...] = total
    send(3, 4, 16, 17)

    def m_plane(d):
        at = pl.ds(pl.multiple_of((own + d) % PLANE * SHARE, 16), SHARE)
        return remote(m1.at[at], pr.at[d], p_s.at[0, d], p_r.at[0, d], plane_dev(d))

    def e_plane(d):
        src = eps.at[(own + d) % PLANE]
        return remote(src, epr.at[d], p_s.at[1, d], p_r.at[1, d], plane_dev(d))

    def start_plane(d, carry):
        e_plane(d).start()
        m_plane(d).start()
        return carry

    lax.fori_loop(1, PLANE, start_plane, 0)
    send(13, 14, 15)

    def sum_e(d, acc):
        e_plane(d).wait_recv()
        return acc + epr[d]

    def sum_m(d, acc):
        m_plane(d).wait_recv()
        return acc + pr[d]

    mine = pl.ds(pl.multiple_of(x * LINE + own * SHARE, 16), SHARE)
    gram_rows = pl.ds(pl.multiple_of(own * 16, 16), 16)
    total = lax.fori_loop(1, PLANE, sum_e, eps[own])
    egs[1, 0:32, :] = total
    g4[block, gram_rows, :] = total[16:32]
    fb[mine, :] = lax.fori_loop(
        1, PLANE, sum_m, m1[pl.ds(pl.multiple_of(own * SHARE, 16), SHARE), :]
    ).astype(BF16)

    def m_share(d):
        return remote(fb.at[mine], fb.at[mine], b_s.at[0, d], b_r.at[0, d], plane_dev(d))

    def g_share(d):
        ref = g4.at[block, gram_rows]
        return remote(ref, ref, b_s.at[1, d], b_r.at[1, d], plane_dev(d))

    def start_share(d, carry):
        m_share(d).start()
        g_share(d).start()
        return carry

    lax.fori_loop(1, PLANE, start_share, 0)
    arrive(0)
    send(5)
    arrive(2)
    send(8, 7)

    def yields_of(i, acc):
        at = pl.ds(pl.multiple_of(i * 128, 128), 128)
        scale = rate[proc[i]] * eff[chan[i]]
        yl = nom[pl.ds(i, 1), :] * scale * jnp.exp(egs[1, pl.ds(i, 1), :])
        ycol[at, :] = jnp.transpose(jnp.broadcast_to(yl, (128, 128)))
        return acc + jnp.dot(
            rows3(yl - obs[pl.ds(i, 1), :]), krow[own, at, :], preferred_element_type=F32
        )

    slope = lax.fori_loop(0, 12, yields_of, jnp.zeros((8, COLS), F32))
    im[0, 256:272, :] = jnp.broadcast_to(slope[0:1] + slope[1:2] + slope[2:3], (16, COLS))

    def wait_plane(d, carry):
        origin = (own + PLANE - d) % PLANE
        ref = fb.at[pl.ds(pl.multiple_of(x * LINE + origin * SHARE, 16), SHARE)]
        remote(ref, ref, b_s.at[0, d], b_r.at[0, d], plane_dev(d)).wait_recv()
        ref = g4.at[block, pl.ds(pl.multiple_of(origin * 16, 16), 16)]
        remote(ref, ref, b_s.at[1, d], b_r.at[1, d], plane_dev(d)).wait_recv()
        return carry

    lax.fori_loop(1, PLANE, wait_plane, 0)

    def m_all(d, at):
        ref = fb.at[line_rows(at)]
        return remote(ref, ref, a_s.at[6 + d], a_r.at[6 + d], line_dev(d))

    for d in range(1, 4):
        m_all(d, x).start()
    g_z = remote(g4.at[block], g4.at[block], x_s.at[6], x_r.at[6], z_mate)
    g_z.start()
    arrive(3)
    send(11)

    def weigh(tiles):
        def step(i, carry):
            at = pl.ds(pl.multiple_of(i * 128, 128), 128)
            yl = ycol[at, :]
            yl = jnp.concatenate([yl, yl], axis=1)
            for p in tiles:
                kc = kcol[tile_x(p), at, :].astype(F32)
                wcol[at, 256 * p : 256 * (p + 1)] = (yl * kc).astype(BF16)
            return carry

        lax.fori_loop(0, 12, step, 0)

    def slot_of(k):
        j = k % 4
        return place(j + j // 2 - 2 * (j // 3), k // 4)

    def half_copy(k, p):
        return remote(pb.at[k, p], precv.at[k, p], e_s.at[k, p], e_r.at[k, p], core_mate)

    def multiply(k, tiles):
        first, count = tiles[0], len(tiles)
        part = dot0(krow[slot_of(k)], wcol[:, 256 * first : 256 * (first + count)])
        for i, p in enumerate(tiles):
            pb[k, p] = part[:, 256 * i : 256 * (i + 1)]

            @pl.when(jnp.logical_not(keeps(p)))
            def _():
                half_copy(k, p).start()

    def out_slot(s, k):
        return part_o.at[s, pl.ds(pl.multiple_of(slot_of(k) * 256, 256), 256)]

    def out_copy(k, p):
        return remote(
            osend.at[k, p], out_slot(zl, k), o_s.at[k, p], o_r.at[zl, k], out_dev(p)
        )

    def own_copy(k, p):
        return pltpu.make_async_copy(osend.at[k, p], out_slot(zl, k), o_r.at[zl, k])

    def hand_out(k, tiles):
        for p in tiles:

            @pl.when(keeps(p))
            def _():
                half_copy(k, p).wait_recv()
                osend[k, p] = (pb[k, p] + precv[k, p]).astype(BF16)

                @pl.when(out_is_self(p))
                def _():
                    own_copy(k, p).start()

                @pl.when(jnp.logical_not(out_is_self(p)))
                def _():
                    out_copy(k, p).start()

    def each(act, blocks, tiles):
        lo, hi = blocks

        def step(k, carry):
            act(k, tiles)
            return carry

        lax.fori_loop(lo, hi, step, 0)

    weigh((0,))
    arrive(1, 13, 14)
    send(6)
    arrive(15)
    send(19, 18)

    arrive(17)
    send(12)

    diag, near, far, every = (0,), (1, 2), (3,), (0, 1, 2, 3)
    each(multiply, (0, 3), diag)
    each(multiply, (4, 5), diag)
    each(hand_out, (0, 3), diag)
    each(hand_out, (4, 5), diag)
    arrive(4, 16)
    weigh(near)
    each(multiply, (0, 3), near)
    each(multiply, (4, 5), near)

    for d in range(1, 4):
        m_all(d, (x + 4 - d) % 4).wait_recv()

    def all_rows(i, carry):
        at = pl.ds(pl.multiple_of(i * 128, 128), 128)
        yl = ycol[at, :]
        vh[at, :] = (jnp.concatenate([yl, yl], axis=1) * fb[at, :].astype(F32)).astype(BF16)
        return carry

    lax.fori_loop(0, 12, all_rows, 0)
    left = dot0(fb[...], vh[:, 0:128])
    c3[0, 0:256, :] = left
    c3[0, 256:384, :] = dot0(fb[:, 128:256], vh[:, 128:256])
    c_half = pl.ds(pl.multiple_of(core * 192, 8), 192)
    i_half = pl.ds(pl.multiple_of(core * 136, 8), 136)
    c_give = pl.ds(pl.multiple_of((1 - core) * 192, 8), 192)
    i_give = pl.ds(pl.multiple_of((1 - core) * 136, 8), 136)

    def swap(buf, slot, half, sem, to):
        src = buf.at[half] if slot is None else buf.at[slot, half]
        dst = buf.at[half] if slot is None else buf.at[slot + 1, half]
        return remote(src, dst, x_s.at[sem], x_r.at[sem], to)

    c_core, c_core_in = (swap(c3, 0, h, 0, core_mate) for h in (c_give, c_half))
    i_core, i_core_in = (swap(im, 0, h, 1, core_mate) for h in (i_give, i_half))
    c_z, i_z = swap(c3, 2, c_half, 2, z_mate), swap(im, 2, i_half, 3, z_mate)
    c_all, c_all_in = (swap(ctot, None, h, 4, core_mate) for h in (c_half, c_give))
    i_all, i_all_in = (swap(itot, None, h, 5, core_mate) for h in (i_half, i_give))
    c_core.start()
    im[0, 0:256, :] = dot0(wcol[:, 0:256], fb[...])
    i_core.start()
    mate = pl.ds((1 - core) * 2, 2)
    pair = pl.ds(core * 2, 2)
    g_z_in = remote(g4.at[core * 2 + 1 - zl], g4.at[core * 2 + 1 - zl], x_s.at[6], x_r.at[6], z_mate)
    g_all = remote(g4.at[pair], g4.at[pair], x_s.at[7], x_r.at[7], core_mate)
    g_all_in = remote(g4.at[mate], g4.at[mate], x_s.at[7], x_r.at[7], core_mate)
    g_z_in.wait_recv()
    g_all.start()

    c_core_in.wait_recv()
    c3[2, c_half, :] = c3[0, c_half, :] + c3[1, c_half, :]
    c_z.start()
    i_core_in.wait_recv()
    im[2, i_half, :] = im[0, i_half, :] + im[1, i_half, :]
    i_z.start()

    each(hand_out, (0, 3), near)
    each(hand_out, (4, 5), near)
    arrive(5, 6)
    each(multiply, (3, 4), (0, 1, 2))
    each(hand_out, (3, 4), (0, 1, 2))
    arrive(7)
    send(9)
    arrive(11, 12)
    weigh(far)
    each(multiply, (0, 4), far)
    arrive(8, 19)
    send(10)
    each(multiply, (4, 5), far)
    each(hand_out, (0, 5), far)

    c_z.wait_recv()
    ctot[c_half, :] = c3[2, c_half, :] + c3[3, c_half, :]
    c_all.start()
    arrive(18)
    each(multiply, (5, 7), every)
    each(hand_out, (5, 7), every)

    c_all_in.wait_recv()
    g_all_in.wait_recv()
    total = ctot[...]
    ab[0:128, 0:128] = total[0:128] + g4[0]
    ab[128:256, 0:128] = total[128:256] + g4[2]
    ab[0:128, 128:256] = jnp.transpose(total[128:256]) + g4[1]
    ab[128:256, 128:256] = total[256:384] + g4[3]
    for i in range(4):
        row, col = 128 * (i // 2), 256 + 128 * (i % 2)
        ab[row : row + 128, col : col + 128] = g4[i]

    def eliminate(i, carry):
        pivot = invert(ab[0:PIV, 0:PIV])
        head = jnp.dot(pivot, ab[0:PIV, :], preferred_element_type=F32, precision=HIGHEST)
        rest = ab[PIV:256, :] - jnp.dot(
            ab[PIV:256, 0:PIV], head, preferred_element_type=F32, precision=HIGHEST
        )
        ab[0 : 256 - PIV, 0:256] = pltpu.roll(rest[:, 0:256], 256 - PIV, 1)
        ab[0 : 256 - PIV, 256:512] = rest[:, 256:512]
        ab[256 - PIV : 256, 0:256] = pltpu.roll(head[:, 0:256], 256 - PIV, 1)
        ab[256 - PIV : 256, 256:512] = head[:, 256:512]
        return carry

    lax.fori_loop(0, 2, eliminate, 0)
    arrive(9, 10)
    each(multiply, (7, 8), every)
    each(hand_out, (7, 8), every)
    lax.fori_loop(2, 4, eliminate, 0)
    i_z.wait_recv()
    itot[i_half, :] = im[2, i_half, :] + im[3, i_half, :]
    i_all.start()
    step = ab[:, 256:512]
    imp_v[...] = jnp.dot(rhs_v, step, preferred_element_type=F32, precision=HIGHEST)
    results = [
        pltpu.make_async_copy(grad_v, grad_o, w_s.at[0]),
        pltpu.make_async_copy(imp_v, imp_o, w_s.at[1]),
        pltpu.make_async_copy(res_v, res_o, w_s.at[2]),
    ]
    results[1].start()
    i_all_in.wait_recv()
    grad_v[...] = itot[256:257, :] + pul[...]
    results[0].start()
    image = rhs_v + itot[0:256, :]
    res_v[...] = rhs_v - jnp.dot(image, step, preferred_element_type=F32, precision=HIGHEST)
    results[2].start()

    def finish(k, carry):
        for s in range(2):
            ref = out_slot(s, k)
            pltpu.make_async_copy(ref, ref, o_r.at[s, k]).wait()
        return carry

    lax.fori_loop(0, 8, finish, 0)

    for d in range(1, 4):
        eg_line(d).wait_send()
        m_line(d).wait_send()
        m_all(d, x).wait_send()

    def drain_plane(d, carry):
        m_plane(d).wait_send()
        e_plane(d).wait_send()
        m_share(d).wait_send()
        g_share(d).wait_send()
        return carry

    lax.fori_loop(1, PLANE, drain_plane, 0)
    for i in range(20):
        copies[i][0]().wait_send()
    for copy in (c_core, c_z, c_all, i_core, i_z, i_all, g_z, g_all):
        copy.wait_send()

    def drain_blocks(k, carry):
        for p in range(4):

            @pl.when(jnp.logical_not(keeps(p)))
            def _():
                half_copy(k, p).wait_send()

            @pl.when(jnp.logical_and(keeps(p), jnp.logical_not(out_is_self(p))))
            def _():
                out_copy(k, p).wait_send()

        return carry

    lax.fori_loop(0, 8, drain_blocks, 0)
    for copy in results:
        copy.wait()


def body(
    log_kappa, block_mask, process, channel, nominal, observed, process_rate, efficiency,
    nuisance_pulls, impact_rhs,
):
    vmem = pl.BlockSpec(memory_space=pltpu.VMEM)
    smem = pl.BlockSpec(memory_space=pltpu.SMEM)
    dma = pltpu.SemaphoreType.DMA
    gradient, parts, impacts, residual = pl.pallas_call(
        kernel,
        name="gauss_newton",
        out_shape=(
            jax.ShapeDtypeStruct((1, COLS), F32),
            jax.ShapeDtypeStruct((2, 2048, COLS), BF16),
            jax.ShapeDtypeStruct((256, 256), F32),
            jax.ShapeDtypeStruct((256, 256), F32),
        ),
        in_specs=[vmem] * 6 + [smem] * 4,
        out_specs=(pl.BlockSpec(memory_space=pl.ANY),) * 4,
        scratch_shapes=[
            pltpu.VMEM((8, ROWS, COLS), BF16),
            pltpu.VMEM((4, ROWS, COLS), BF16),
            pltpu.VMEM((ROWS, 1024), BF16),
            pltpu.VMEM((ROWS, COLS), BF16),
            pltpu.VMEM((3, LINE, COLS), BF16),
            pltpu.VMEM((LINE, COLS), F32),
            pltpu.VMEM((PLANE, SHARE, COLS), F32),
            pltpu.VMEM((ROWS, COLS), BF16),
            pltpu.VMEM((ROWS, 128), F32),
            pltpu.VMEM((ROWS, COLS), BF16),
            pltpu.VMEM((512, 128), F32),
            pltpu.VMEM((4, 128, 128), F32),
            pltpu.VMEM((2, 144, 128), F32),
            pltpu.VMEM((3, 144, 128), F32),
            pltpu.VMEM((PLANE, 32, 128), F32),
            pltpu.VMEM((PLANE, 32, 128), F32),
            pltpu.VMEM((4, 384, 128), F32),
            pltpu.VMEM((4, 272, COLS), F32),
            pltpu.VMEM((256, 512), F32),
            pltpu.VMEM((8, 4, 256, 256), F32),
            pltpu.VMEM((8, 4, 256, 256), F32),
            pltpu.VMEM((8, 4, 256, 256), BF16),
            pltpu.VMEM((384, 128), F32),
            pltpu.VMEM((272, COLS), F32),
            pltpu.VMEM((1, COLS), F32),
            pltpu.VMEM((256, 256), F32),
            pltpu.VMEM((256, 256), F32),
            dma((10,)), dma((10,)), dma((2, PLANE)), dma((2, PLANE)), dma((2, PLANE)), dma((2, PLANE)),
            dma((20,)), dma((20,)), dma((8,)), dma((8,)), dma((3,)),
            dma((8, 4)), dma((8, 4)), dma((8, 4)), dma((2, 8)),
        ],
        compiler_params=pltpu.CompilerParams(
            collective_id=0, has_side_effects=True, vmem_limit_bytes=62 * 2**20
        ),
    )(
        log_kappa, block_mask, nominal.reshape(12, 128), observed.reshape(12, 128),
        nuisance_pulls.reshape(1, COLS), impact_rhs, process, channel, process_rate, efficiency,
    )
    tile_rows = 8 * 256
    row = lax.axis_index("bins") * tile_rows + lax.broadcasted_iota(jnp.int32, (tile_rows, COLS), 0)
    col = lax.axis_index("nuis") * COLS + lax.broadcasted_iota(jnp.int32, (tile_rows, COLS), 1)
    first, second = (parts[s].astype(F32) for s in range(2))
    hessian = first + second + (row == col).astype(F32)
    return gradient.reshape(COLS), hessian, impacts, residual


def solution(mesh):
    in_specs = (
        P("bins", "nuis"),
        P("bins", "nuis"),
        P("bins"),
        P("bins"),
        P("bins"),
        P("bins"),
        P(),
        P(),
        P("nuis"),
        P("nuis", None),
    )
    out_specs = (P("nuis"), P("bins", "nuis"), P("nuis", None), P("nuis", None))
    return jax.shard_map(body, mesh=mesh, in_specs=in_specs, out_specs=out_specs, check_vma=False)
```

```python
import jax
import jax.numpy as jnp
from jax import lax
from jax.experimental import pallas as pl
from jax.experimental.pallas import tpu as pltpu
from jax.sharding import PartitionSpec as P

MESH = pl.DeviceIdType.MESH
F32, BF16 = jnp.float32, jnp.bfloat16
HIGHEST = lax.Precision.HIGHEST
ROWS, COLS, SHARE, PLANE = 1536, 256, 48, 8
HALF = ROWS // 2
FIRST = 1280
LINE = ROWS // 4
PIV, PANEL = 64, 8


def dot0(a, b, precision=None):
    return lax.dot_general(
        a, b, (((0,), (0,)), ((), ())), preferred_element_type=F32, precision=precision
    )


def split2(v):
    hi = v.astype(BF16).astype(F32)
    return hi, (v - hi).astype(BF16).astype(F32)


def split3(v):
    hi, mid = split2(v)
    return hi, mid, (v - hi) - mid


def lane_of(rows, lanes=128):
    return lax.broadcasted_iota(jnp.int32, (rows, lanes), 1)


def invert(block):
    lane = lax.broadcasted_iota(jnp.int32, (PIV, PIV), 1)
    sub = lax.broadcasted_iota(jnp.int32, (PIV, PIV), 0)
    wide = lax.broadcasted_iota(jnp.int32, (PIV, 128), 0)
    for first in range(0, PIV, PANEL):
        cols = [
            jnp.broadcast_to(block[:, first + k : first + k + 1], (PIV, 128)) for k in range(PANEL)
        ]
        used = []
        for j in range(PANEL):
            at, col = first + j, cols[j]
            inv = 1.0 / col[at : at + 1, :]
            used.append((col, inv))
            for k in range(PANEL):
                if k != j:
                    row = cols[k][at : at + 1, :] * inv
                    cols[k] = jnp.where(wide == at, row, cols[k] - col * row)
            cols[j] = jnp.where(wide == at, inv, -col * inv)
        for j in range(PANEL):
            at, (col, inv) = first + j, used[j]
            row = block[at : at + 1, :] * inv[:, 0:PIV]
            block = jnp.where(sub == at, row, block - col[:, 0:PIV] * row)
        for k in range(PANEL):
            block = jnp.where(lane == first + k, cols[k][:, 0:PIV], block)
    return block


def rows3(v):
    hi, mid, low = split3(v)
    r = lax.broadcasted_iota(jnp.int32, (8, v.shape[1]), 0)
    out = jnp.where(r == 0, hi, jnp.where(r == 1, mid, jnp.where(r == 2, low, 0.0)))
    return out.astype(BF16)


def kernel(
    lk, mask, nom, obs, pul, rhs, proc, chan, rate, eff,
    grad_o, part_o, imp_o, res_o,
    krow, kcol, wcol, sb, xr, m1, pr, fb, ycol, vh, gt, g4, egs, egx, eps, epr, c3, im, ab,
    pb, precv, osend, ctot, itot, grad_v, imp_v, res_v,
    g_s, g_r, k_s, k_r, x_s, x_r, w_s, e_s, e_r, o_s, o_r,
):
    n = lax.axis_index("nuis")
    b = lax.axis_index("bins")
    x, y, zh = n // 8, (n // 2) % 4, n % 2
    zl, core = b // 2, b % 2

    def dev(dx=0, dy=0, dz=0):
        return {"nuis": ((x + dx) % 4) * 8 + ((y + dy) % 4) * 2 + (zh + dz) % 2, "bins": b}

    def place(dy=0, dz=0):
        return ((y + dy) % 4) * 2 + (zh + dz) % 2

    def remote(src, dst, s, r, to):
        return pltpu.make_async_remote_copy(
            src_ref=src, dst_ref=dst, send_sem=s, recv_sem=r, device_id=to, device_id_type=MESH
        )

    def wait_all(ref, sem):
        pltpu.make_async_copy(ref, ref, sem).wait()

    own = place()
    block = core * 2 + zl

    def line_dev(d):
        return {"nuis": ((x + d) % 4) * PLANE + own, "bins": b}

    def plane_dev(d):
        return {"nuis": x * PLANE + (own + d) % PLANE, "bins": b}

    core_mate = {"nuis": n, "bins": zl * 2 + (1 - core)}
    z_mate = {"nuis": n, "bins": (1 - zl) * 2 + core}

    steps = (0, 1, 3, 2)

    def tile_x(p):
        return (x + steps[p]) % 4

    def keeps(p):
        return tile_x(p) // 2 == core

    def out_dev(p):
        return {"nuis": tile_x(p) * 8 + y * 2 + zh, "bins": x}

    def out_is_self(p):
        return jnp.logical_and(tile_x(p) == x, x == b)

    def in_dev(s):
        return {"nuis": b * 8 + y * 2 + zh, "bins": 2 * s + x // 2}

    def in_is_self(s):
        return jnp.logical_and(b == x, 2 * s + x // 2 == b)

    bar = pltpu.get_barrier_semaphore()

    def greet_line(d, carry):
        pl.semaphore_signal(bar, inc=1, device_id=line_dev(d), device_id_type=MESH)
        return carry

    def greet_plane(d, carry):
        pl.semaphore_signal(bar, inc=1, device_id=plane_dev(d), device_id_type=MESH)
        return carry

    lax.fori_loop(1, 4, greet_line, 0)
    lax.fori_loop(1, PLANE, greet_plane, 0)
    for mate in (core_mate, z_mate):
        pl.semaphore_signal(bar, inc=1, device_id=mate, device_id_type=MESH)
    expected = jnp.int32(3 + PLANE - 1 + 2)
    others = [(out_dev(p), jnp.logical_and(keeps(p), jnp.logical_not(out_is_self(p)))) for p in range(4)]
    others += [(in_dev(s), jnp.logical_not(in_is_self(s))) for s in range(2)]
    for other, wanted in others:

        @pl.when(wanted)
        def _():
            pl.semaphore_signal(bar, inc=1, device_id=other, device_id_type=MESH)

        expected = expected + jnp.where(wanted, 1, 0)

    rhs_v = rhs[...]
    r_hi, r_mid = split2(rhs_v)
    r_hi, r_mid = r_hi.astype(BF16), r_mid.astype(BF16)
    pulls = rows3(pul[...])
    egs[0, 128:144, :] = jnp.zeros((16, 128), F32)

    def own_rows(i, carry):
        at = pl.ds(pl.multiple_of(i * 128, 128), 128)
        kb = lk[at, :] * mask[pl.ds(i, 1), :].astype(F32).astype(BF16)
        krow[own, at, :] = kb
        kcol[x, at, :] = kb
        e = lax.dot_general(pulls, kb, (((1,), (1,)), ((), ())), preferred_element_type=F32)
        egs[0, pl.ds(128 + i, 1), :] = e[0:1] + e[1:2] + e[2:3]
        m = jnp.dot(kb, r_hi, preferred_element_type=F32) + jnp.dot(
            kb, r_mid, preferred_element_type=F32
        )
        sb[at, :] = m.astype(BF16)
        return carry

    lax.fori_loop(0, 12, own_rows, 0)

    gram = dot0(rhs_v, rhs_v, HIGHEST)
    gt[0:256, :] = gram[:, 0:128]
    gt[256:512, :] = gram[:, 128:256]
    egs[0, 0:128, :] = gt[pl.ds(pl.multiple_of(b * 128, 128), 128), :]

    pl.semaphore_wait(bar, expected)

    def line_rows(at):
        return pl.ds(pl.multiple_of(at * LINE, 16), LINE)

    def m_line(d):
        return remote(
            sb.at[line_rows((x + d) % 4)], xr.at[d - 1], g_s.at[0], g_r.at[0], line_dev(d)
        )

    def eg_line(d):
        return remote(egs.at[0], egx.at[d - 1], g_s.at[1], g_r.at[1], line_dev(d))

    for d in range(1, 4):
        eg_line(d).start()
    for d in range(1, 4):
        m_line(d).start()

    def row_copy(i, slot, to, lo=0, size=ROWS):
        ref = krow.at[slot, pl.ds(lo, size)]
        return remote(ref, ref, k_s.at[0], k_r.at[i], to)

    def col_copy(i, slot, to, lo=0, size=ROWS):
        ref = kcol.at[slot, pl.ds(lo, size)]
        return remote(ref, ref, k_s.at[1], k_r.at[i], to)

    up_x, down_x = (x + 1) % 4, (x + 3) % 4
    far_x = (x + 2) % 4
    rest = ROWS - FIRST
    copies = {
        0: (lambda: row_copy(0, own, dev(dy=1), 0, FIRST),
            lambda: row_copy(0, place(3), dev(dy=3), 0, FIRST)),
        1: (lambda: row_copy(1, own, dev(dy=3), 0, FIRST),
            lambda: row_copy(1, place(1), dev(dy=1), 0, FIRST)),
        2: (lambda: row_copy(2, own, dev(dz=1), 0, FIRST),
            lambda: row_copy(2, place(0, 1), dev(dz=1), 0, FIRST)),
        3: (lambda: col_copy(3, x, dev(dx=1), 0, HALF),
            lambda: col_copy(3, down_x, dev(dx=3), 0, HALF)),
        4: (lambda: col_copy(4, x, dev(dx=3), 0, HALF),
            lambda: col_copy(4, up_x, dev(dx=1), 0, HALF)),
        13: (lambda: row_copy(13, own, dev(dy=1), FIRST, rest),
             lambda: row_copy(13, place(3), dev(dy=3), FIRST, rest)),
        14: (lambda: row_copy(14, own, dev(dy=3), FIRST, rest),
             lambda: row_copy(14, place(1), dev(dy=1), FIRST, rest)),
        15: (lambda: row_copy(15, own, dev(dz=1), FIRST, rest),
             lambda: row_copy(15, place(0, 1), dev(dz=1), FIRST, rest)),
        16: (lambda: col_copy(16, x, dev(dx=1), HALF, HALF),
             lambda: col_copy(16, down_x, dev(dx=3), HALF, HALF)),
        17: (lambda: col_copy(17, x, dev(dx=3), HALF, HALF),
             lambda: col_copy(17, up_x, dev(dx=1), HALF, HALF)),
        5: (lambda: row_copy(5, place(3), dev(dy=1), 0, HALF),
            lambda: row_copy(5, place(2), dev(dy=3), 0, HALF)),
        6: (lambda: row_copy(6, place(1), dev(dy=3), HALF, HALF),
            lambda: row_copy(6, place(2), dev(dy=1), HALF, HALF)),
        7: (lambda: row_copy(7, place(0, 1), dev(dy=1), 0, FIRST),
            lambda: row_copy(7, place(3, 1), dev(dy=3), 0, FIRST)),
        8: (lambda: row_copy(8, place(0, 1), dev(dy=3), 0, FIRST),
            lambda: row_copy(8, place(1, 1), dev(dy=1), 0, FIRST)),
        18: (lambda: row_copy(18, place(0, 1), dev(dy=1), FIRST, rest),
             lambda: row_copy(18, place(3, 1), dev(dy=3), FIRST, rest)),
        19: (lambda: row_copy(19, place(0, 1), dev(dy=3), FIRST, rest),
             lambda: row_copy(19, place(1, 1), dev(dy=1), FIRST, rest)),
        9: (lambda: row_copy(9, place(3, 1), dev(dy=1), 0, HALF),
            lambda: row_copy(9, place(2, 1), dev(dy=3), 0, HALF)),
        10: (lambda: row_copy(10, place(1, 1), dev(dy=3), HALF, HALF),
             lambda: row_copy(10, place(2, 1), dev(dy=1), HALF, HALF)),
        11: (lambda: col_copy(11, down_x, dev(dx=1), 0, HALF),
             lambda: col_copy(11, far_x, dev(dx=3), 0, HALF)),
        12: (lambda: col_copy(12, up_x, dev(dx=3), HALF, HALF),
             lambda: col_copy(12, far_x, dev(dx=1), HALF, HALF)),
    }

    def send(*which):
        for i in which:
            copies[i][0]().start()

    def arrive(*which):
        for i in which:
            copies[i][1]().wait_recv()

    send(0, 1, 2)

    wait_all(egx, g_r.at[1])
    total = egs[0]
    for d in range(1, 4):
        total = total + egx[d - 1]
    for q in range(PLANE):
        eps[q, 0:16, :] = total[128:144]
        eps[q, 16:32, :] = total[16 * q : 16 * (q + 1)]
    line = line_rows(x)
    wait_all(xr, g_r.at[0])
    total = sb[line, :].astype(F32)
    for d in range(1, 4):
        total = total + xr[d - 1].astype(F32)
    m1[...] = total
    send(3, 4, 16, 17)

    def m_plane(d):
        at = pl.ds(pl.multiple_of((own + d) % PLANE * SHARE, 16), SHARE)
        return remote(m1.at[at], pr.at[d], g_s.at[3], g_r.at[3], plane_dev(d))

    def e_plane(d):
        src = eps.at[(own + d) % PLANE]
        return remote(src, epr.at[d], g_s.at[4], g_r.at[4], plane_dev(d))

    def start_plane(d, carry):
        e_plane(d).start()
        m_plane(d).start()
        return carry

    lax.fori_loop(1, PLANE, start_plane, 0)
    send(13, 14, 15)

    def sum_e(d, acc):
        return acc + epr[d]

    def sum_m(d, acc):
        return acc + pr[d]

    mine = pl.ds(pl.multiple_of(x * LINE + own * SHARE, 16), SHARE)
    gram_rows = pl.ds(pl.multiple_of(own * 16, 16), 16)
    wait_all(epr.at[pl.ds(1, PLANE - 1)], g_r.at[4])
    total = lax.fori_loop(1, PLANE, sum_e, eps[own])
    egs[1, 0:32, :] = total
    g4[block, gram_rows, :] = total[16:32]
    wait_all(pr.at[pl.ds(1, PLANE - 1)], g_r.at[3])
    fb[mine, :] = lax.fori_loop(
        1, PLANE, sum_m, m1[pl.ds(pl.multiple_of(own * SHARE, 16), SHARE), :]
    ).astype(BF16)

    def m_share(d):
        return remote(fb.at[mine], fb.at[mine], g_s.at[5], g_r.at[5], plane_dev(d))

    def g_share(d):
        ref = g4.at[block, gram_rows]
        return remote(ref, ref, g_s.at[6], g_r.at[6], plane_dev(d))

    def start_share(d, carry):
        m_share(d).start()
        g_share(d).start()
        return carry

    lax.fori_loop(1, PLANE, start_share, 0)
    arrive(0)
    send(5)
    arrive(2)
    send(8, 7)

    def yields_of(i, acc):
        at = pl.ds(pl.multiple_of(i * 128, 128), 128)
        scale = rate[proc[i]] * eff[chan[i]]
        yl = nom[pl.ds(i, 1), :] * scale * jnp.exp(egs[1, pl.ds(i, 1), :])
        ycol[at, :] = jnp.transpose(jnp.broadcast_to(yl, (128, 128)))
        return acc + jnp.dot(
            rows3(yl - obs[pl.ds(i, 1), :]), krow[own, at, :], preferred_element_type=F32
        )

    slope = lax.fori_loop(0, 12, yields_of, jnp.zeros((8, COLS), F32))
    im[0, 256:272, :] = jnp.broadcast_to(slope[0:1] + slope[1:2] + slope[2:3], (16, COLS))

    wait_all(fb.at[pl.ds(0, (PLANE - 1) * SHARE)], g_r.at[5])
    wait_all(g4.at[0, pl.ds(0, (PLANE - 1) * 16)], g_r.at[6])

    def m_all(d, at):
        ref = fb.at[line_rows(at)]
        return remote(ref, ref, g_s.at[2], g_r.at[2], line_dev(d))

    for d in range(1, 4):
        m_all(d, x).start()
    g_z = remote(g4.at[block], g4.at[block], x_s.at[6], x_r.at[6], z_mate)
    g_z.start()
    arrive(3)
    send(11)

    def weigh(tiles):
        def step(i, carry):
            at = pl.ds(pl.multiple_of(i * 128, 128), 128)
            yl = ycol[at, :]
            yl = jnp.concatenate([yl, yl], axis=1)
            for p in tiles:
                kc = kcol[tile_x(p), at, :].astype(F32)
                wcol[at, 256 * p : 256 * (p + 1)] = (yl * kc).astype(BF16)
            return carry

        lax.fori_loop(0, 12, step, 0)

    def slot_of(k):
        j = k % 4
        return place(j + j // 2 - 2 * (j // 3), k // 4)

    def half_copy(k, p):
        return remote(pb.at[k, p], precv.at[k, p], e_s.at[p], e_r.at[k, tile_x(p) % 2], core_mate)

    def multiply(k, tiles):
        first, count = tiles[0], len(tiles)
        part = dot0(krow[slot_of(k)], wcol[:, 256 * first : 256 * (first + count)])
        for i, p in enumerate(tiles):
            pb[k, p] = part[:, 256 * i : 256 * (i + 1)]

            @pl.when(jnp.logical_not(keeps(p)))
            def _():
                half_copy(k, p).start()

    def out_slot(s, k):
        return part_o.at[s, pl.ds(pl.multiple_of(slot_of(k) * 256, 256), 256)]

    def out_copy(k, p):
        return remote(
            osend.at[k, p], out_slot(zl, k), o_s.at[p], o_r.at[zl, k], out_dev(p)
        )

    def own_copy(k, p):
        return pltpu.make_async_copy(osend.at[k, p], out_slot(zl, k), o_r.at[zl, k])

    def hand_out(k, tiles):
        for p in tiles:

            @pl.when(keeps(p))
            def _():
                half_copy(k, p).wait_recv()
                osend[k, p] = (pb[k, p] + precv[k, p]).astype(BF16)

                @pl.when(out_is_self(p))
                def _():
                    own_copy(k, p).start()

                @pl.when(jnp.logical_not(out_is_self(p)))
                def _():
                    out_copy(k, p).start()

    def each(act, blocks, tiles):
        lo, hi = blocks

        def step(k, carry):
            act(k, tiles)
            return carry

        lax.fori_loop(lo, hi, step, 0)

    weigh((0,))
    arrive(1, 13, 14)
    send(6)
    arrive(15)
    send(19, 18)

    arrive(17)
    send(12)

    diag, near, far, every = (0,), (1, 2), (3,), (0, 1, 2, 3)
    each(multiply, (0, 3), diag)
    each(multiply, (4, 5), diag)
    each(hand_out, (0, 3), diag)
    each(hand_out, (4, 5), diag)
    arrive(4, 16)
    weigh(near)
    each(multiply, (0, 3), near)
    each(multiply, (4, 5), near)

    wait_all(fb.at[pl.ds(0, 3 * LINE)], g_r.at[2])

    def all_rows(i, carry):
        at = pl.ds(pl.multiple_of(i * 128, 128), 128)
        yl = ycol[at, :]
        vh[at, :] = (jnp.concatenate([yl, yl], axis=1) * fb[at, :].astype(F32)).astype(BF16)
        return carry

    lax.fori_loop(0, 12, all_rows, 0)
    left = dot0(fb[...], vh[:, 0:128])
    c3[0, 0:256, :] = left
    c3[0, 256:384, :] = dot0(fb[:, 128:256], vh[:, 128:256])
    c_half = pl.ds(pl.multiple_of(core * 192, 8), 192)
    i_half = pl.ds(pl.multiple_of(core * 136, 8), 136)
    c_give = pl.ds(pl.multiple_of((1 - core) * 192, 8), 192)
    i_give = pl.ds(pl.multiple_of((1 - core) * 136, 8), 136)

    def swap(buf, slot, half, sem, to):
        src = buf.at[half] if slot is None else buf.at[slot, half]
        dst = buf.at[half] if slot is None else buf.at[slot + 1, half]
        return remote(src, dst, x_s.at[sem], x_r.at[sem], to)

    c_core, c_core_in = (swap(c3, 0, h, 0, core_mate) for h in (c_give, c_half))
    i_core, i_core_in = (swap(im, 0, h, 1, core_mate) for h in (i_give, i_half))
    c_z, i_z = swap(c3, 2, c_half, 2, z_mate), swap(im, 2, i_half, 3, z_mate)
    c_all, c_all_in = (swap(ctot, None, h, 4, core_mate) for h in (c_half, c_give))
    i_all, i_all_in = (swap(itot, None, h, 5, core_mate) for h in (i_half, i_give))
    c_core.start()
    im[0, 0:256, :] = dot0(wcol[:, 0:256], fb[...])
    i_core.start()
    mate = pl.ds((1 - core) * 2, 2)
    pair = pl.ds(core * 2, 2)
    g_z_in = remote(g4.at[core * 2 + 1 - zl], g4.at[core * 2 + 1 - zl], x_s.at[6], x_r.at[6], z_mate)
    g_all = remote(g4.at[pair], g4.at[pair], x_s.at[7], x_r.at[7], core_mate)
    g_all_in = remote(g4.at[mate], g4.at[mate], x_s.at[7], x_r.at[7], core_mate)
    g_z_in.wait_recv()
    g_all.start()

    c_core_in.wait_recv()
    c3[2, c_half, :] = c3[0, c_half, :] + c3[1, c_half, :]
    c_z.start()
    i_core_in.wait_recv()
    im[2, i_half, :] = im[0, i_half, :] + im[1, i_half, :]
    i_z.start()

    arrive(11, 12)
    weigh(far)
    each(multiply, (0, 3), far)
    each(multiply, (4, 5), far)

    c_z.wait_recv()
    ctot[c_half, :] = c3[2, c_half, :] + c3[3, c_half, :]
    c_all.start()
    each(hand_out, (0, 3), near)
    each(hand_out, (4, 5), near)
    arrive(7)
    send(9)
    arrive(8, 19)
    send(10)
    each(hand_out, (0, 3), far)
    each(hand_out, (4, 5), far)
    arrive(5, 6)
    each(multiply, (3, 4), every)
    each(hand_out, (3, 4), every)

    c_all_in.wait_recv()
    g_all_in.wait_recv()
    total = ctot[...]
    ab[0:128, 0:128] = total[0:128] + g4[0]
    ab[128:256, 0:128] = total[128:256] + g4[2]
    ab[0:128, 128:256] = jnp.transpose(total[128:256]) + g4[1]
    ab[128:256, 128:256] = total[256:384] + g4[3]
    for i in range(4):
        row, col = 128 * (i // 2), 256 + 128 * (i % 2)
        ab[row : row + 128, col : col + 128] = g4[i]

    def eliminate(i, carry):
        pivot = invert(ab[0:PIV, 0:PIV])
        head = jnp.dot(pivot, ab[0:PIV, :], preferred_element_type=F32, precision=HIGHEST)
        rest = ab[PIV:256, :] - jnp.dot(
            ab[PIV:256, 0:PIV], head, preferred_element_type=F32, precision=HIGHEST
        )
        ab[0 : 256 - PIV, 0:256] = pltpu.roll(rest[:, 0:256], 256 - PIV, 1)
        ab[0 : 256 - PIV, 256:512] = rest[:, 256:512]
        ab[256 - PIV : 256, 0:256] = pltpu.roll(head[:, 0:256], 256 - PIV, 1)
        ab[256 - PIV : 256, 256:512] = head[:, 256:512]
        return carry

    lax.fori_loop(0, 2, eliminate, 0)
    arrive(18)
    each(multiply, (5, 7), every)
    each(hand_out, (5, 7), every)
    arrive(9, 10)
    each(multiply, (7, 8), every)
    each(hand_out, (7, 8), every)
    lax.fori_loop(2, 4, eliminate, 0)
    i_z.wait_recv()
    itot[i_half, :] = im[2, i_half, :] + im[3, i_half, :]
    i_all.start()
    step = ab[:, 256:512]
    imp_v[...] = jnp.dot(rhs_v, step, preferred_element_type=F32, precision=HIGHEST)
    results = [
        pltpu.make_async_copy(grad_v, grad_o, w_s.at[0]),
        pltpu.make_async_copy(imp_v, imp_o, w_s.at[1]),
        pltpu.make_async_copy(res_v, res_o, w_s.at[2]),
    ]
    results[1].start()
    i_all_in.wait_recv()
    grad_v[...] = itot[256:257, :] + pul[...]
    results[0].start()
    image = rhs_v + itot[0:256, :]
    res_v[...] = rhs_v - jnp.dot(image, step, preferred_element_type=F32, precision=HIGHEST)
    results[2].start()

    def finish(k, carry):
        for s in range(2):
            ref = out_slot(s, k)
            pltpu.make_async_copy(ref, ref, o_r.at[s, k]).wait()
        return carry

    lax.fori_loop(0, 8, finish, 0)

    wait_all(xr, g_s.at[0])
    wait_all(egx, g_s.at[1])
    wait_all(fb.at[pl.ds(0, 3 * LINE)], g_s.at[2])
    wait_all(pr.at[pl.ds(1, PLANE - 1)], g_s.at[3])
    wait_all(epr.at[pl.ds(1, PLANE - 1)], g_s.at[4])
    wait_all(fb.at[pl.ds(0, (PLANE - 1) * SHARE)], g_s.at[5])
    wait_all(g4.at[0, pl.ds(0, (PLANE - 1) * 16)], g_s.at[6])
    wait_all(krow.at[pl.ds(0, 7)], k_s.at[0])
    wait_all(kcol.at[pl.ds(0, 3)], k_s.at[1])
    for copy in (c_core, c_z, c_all, i_core, i_z, i_all, g_z, g_all):
        copy.wait_send()

    for p in range(4):

        @pl.when(jnp.logical_not(keeps(p)))
        def _():
            wait_all(pb.at[:, p], e_s.at[p])

        @pl.when(jnp.logical_and(keeps(p), jnp.logical_not(out_is_self(p))))
        def _():
            wait_all(osend.at[:, p], o_s.at[p])

    for copy in results:
        copy.wait()


def body(
    log_kappa, block_mask, process, channel, nominal, observed, process_rate, efficiency,
    nuisance_pulls, impact_rhs,
):
    vmem = pl.BlockSpec(memory_space=pltpu.VMEM)
    smem = pl.BlockSpec(memory_space=pltpu.SMEM)
    dma = pltpu.SemaphoreType.DMA
    gradient, parts, impacts, residual = pl.pallas_call(
        kernel,
        name="gauss_newton",
        out_shape=(
            jax.ShapeDtypeStruct((1, COLS), F32),
            jax.ShapeDtypeStruct((2, 2048, COLS), BF16),
            jax.ShapeDtypeStruct((256, 256), F32),
            jax.ShapeDtypeStruct((256, 256), F32),
        ),
        in_specs=[vmem] * 6 + [smem] * 4,
        out_specs=(pl.BlockSpec(memory_space=pl.ANY),) * 4,
        scratch_shapes=[
            pltpu.VMEM((8, ROWS, COLS), BF16),
            pltpu.VMEM((4, ROWS, COLS), BF16),
            pltpu.VMEM((ROWS, 1024), BF16),
            pltpu.VMEM((ROWS, COLS), BF16),
            pltpu.VMEM((3, LINE, COLS), BF16),
            pltpu.VMEM((LINE, COLS), F32),
            pltpu.VMEM((PLANE, SHARE, COLS), F32),
            pltpu.VMEM((ROWS, COLS), BF16),
            pltpu.VMEM((ROWS, 128), F32),
            pltpu.VMEM((ROWS, COLS), BF16),
            pltpu.VMEM((512, 128), F32),
            pltpu.VMEM((4, 128, 128), F32),
            pltpu.VMEM((2, 144, 128), F32),
            pltpu.VMEM((3, 144, 128), F32),
            pltpu.VMEM((PLANE, 32, 128), F32),
            pltpu.VMEM((PLANE, 32, 128), F32),
            pltpu.VMEM((4, 384, 128), F32),
            pltpu.VMEM((4, 272, COLS), F32),
            pltpu.VMEM((256, 512), F32),
            pltpu.VMEM((8, 4, 256, 256), F32),
            pltpu.VMEM((8, 4, 256, 256), F32),
            pltpu.VMEM((8, 4, 256, 256), BF16),
            pltpu.VMEM((384, 128), F32),
            pltpu.VMEM((272, COLS), F32),
            pltpu.VMEM((1, COLS), F32),
            pltpu.VMEM((256, 256), F32),
            pltpu.VMEM((256, 256), F32),
            dma((7,)), dma((7,)), dma((2,)), dma((20,)), dma((8,)), dma((8,)), dma((3,)),
            dma((4,)), dma((8, 2)), dma((4,)), dma((2, 8)),
        ],
        compiler_params=pltpu.CompilerParams(
            collective_id=0, has_side_effects=True, vmem_limit_bytes=62 * 2**20
        ),
    )(
        log_kappa, block_mask, nominal.reshape(12, 128), observed.reshape(12, 128),
        nuisance_pulls.reshape(1, COLS), impact_rhs, process, channel, process_rate, efficiency,
    )
    tile_rows = 8 * 256
    row = lax.axis_index("bins") * tile_rows + lax.broadcasted_iota(jnp.int32, (tile_rows, COLS), 0)
    col = lax.axis_index("nuis") * COLS + lax.broadcasted_iota(jnp.int32, (tile_rows, COLS), 1)
    first, second = (parts[s].astype(F32) for s in range(2))
    hessian = first + second + (row == col).astype(F32)
    return gradient.reshape(COLS), hessian, impacts, residual


def solution(mesh):
    in_specs = (
        P("bins", "nuis"),
        P("bins", "nuis"),
        P("bins"),
        P("bins"),
        P("bins"),
        P("bins"),
        P(),
        P(),
        P("nuis"),
        P("nuis", None),
    )
    out_specs = (P("nuis"), P("bins", "nuis"), P("nuis", None), P("nuis", None))
    return jax.shard_map(body, mesh=mesh, in_specs=in_specs, out_specs=out_specs, check_vma=False)
```

```python
import jax
import jax.numpy as jnp
from jax import lax
from jax.experimental import pallas as pl
from jax.experimental.pallas import tpu as pltpu
from jax.sharding import PartitionSpec as P

MESH = pl.DeviceIdType.MESH
F32, BF16 = jnp.float32, jnp.bfloat16
HIGHEST = lax.Precision.HIGHEST
ROWS, COLS, SHARE, PLANE = 1536, 256, 48, 8
HALF = ROWS // 2
FIRST = 1280
LINE = ROWS // 4
PIV, PANEL = 64, 8


def dot0(a, b, precision=None):
    return lax.dot_general(
        a, b, (((0,), (0,)), ((), ())), preferred_element_type=F32, precision=precision
    )


def split2(v):
    hi = v.astype(BF16).astype(F32)
    return hi, (v - hi).astype(BF16).astype(F32)


def split3(v):
    hi, mid = split2(v)
    return hi, mid, (v - hi) - mid


def lane_of(rows, lanes=128):
    return lax.broadcasted_iota(jnp.int32, (rows, lanes), 1)


def invert(block):
    lane = lax.broadcasted_iota(jnp.int32, (PIV, PIV), 1)
    sub = lax.broadcasted_iota(jnp.int32, (PIV, PIV), 0)
    wide = lax.broadcasted_iota(jnp.int32, (PIV, 128), 0)
    for first in range(0, PIV, PANEL):
        cols = [
            jnp.broadcast_to(block[:, first + k : first + k + 1], (PIV, 128)) for k in range(PANEL)
        ]
        used = []
        for j in range(PANEL):
            at, col = first + j, cols[j]
            inv = 1.0 / col[at : at + 1, :]
            used.append((col, inv))
            for k in range(PANEL):
                if k != j:
                    row = cols[k][at : at + 1, :] * inv
                    cols[k] = jnp.where(wide == at, row, cols[k] - col * row)
            cols[j] = jnp.where(wide == at, inv, -col * inv)
        for j in range(PANEL):
            at, (col, inv) = first + j, used[j]
            row = block[at : at + 1, :] * inv[:, 0:PIV]
            block = jnp.where(sub == at, row, block - col[:, 0:PIV] * row)
        for k in range(PANEL):
            block = jnp.where(lane == first + k, cols[k][:, 0:PIV], block)
    return block


def rows3(v):
    hi, mid, low = split3(v)
    r = lax.broadcasted_iota(jnp.int32, (8, v.shape[1]), 0)
    out = jnp.where(r == 0, hi, jnp.where(r == 1, mid, jnp.where(r == 2, low, 0.0)))
    return out.astype(BF16)


def kernel(
    lk, mask, nom, obs, pul, rhs, proc, chan, rate, eff,
    grad_o, part_o, imp_o, res_o,
    krow, kcol, wcol, sb, xr, m1, pr, fb, ycol, vh, gt, g4, egs, egx, eps, epr, c3, im, ab,
    pb, precv, osend, ctot, itot, grad_v, imp_v, res_v,
    g_s, g_r, k_s, k_r, x_s, x_r, w_s, e_s, e_r, o_s, o_r,
):
    n = lax.axis_index("nuis")
    b = lax.axis_index("bins")
    x, y, zh = n // 8, (n // 2) % 4, n % 2
    zl, core = b // 2, b % 2

    def dev(dx=0, dy=0, dz=0):
        return {"nuis": ((x + dx) % 4) * 8 + ((y + dy) % 4) * 2 + (zh + dz) % 2, "bins": b}

    def place(dy=0, dz=0):
        return ((y + dy) % 4) * 2 + (zh + dz) % 2

    def remote(src, dst, s, r, to):
        return pltpu.make_async_remote_copy(
            src_ref=src, dst_ref=dst, send_sem=s, recv_sem=r, device_id=to, device_id_type=MESH
        )

    def wait_all(ref, sem):
        pltpu.make_async_copy(ref, ref, sem).wait()

    own = place()
    block = core * 2 + zl

    def line_dev(d):
        return {"nuis": ((x + d) % 4) * PLANE + own, "bins": b}

    def plane_dev(d):
        return {"nuis": x * PLANE + (own + d) % PLANE, "bins": b}

    core_mate = {"nuis": n, "bins": zl * 2 + (1 - core)}
    z_mate = {"nuis": n, "bins": (1 - zl) * 2 + core}

    steps = (0, 1, 3, 2)

    def tile_x(p):
        return (x + steps[p]) % 4

    def keeps(p):
        return tile_x(p) // 2 == core

    def out_dev(p):
        return {"nuis": tile_x(p) * 8 + y * 2 + zh, "bins": x}

    def out_is_self(p):
        return jnp.logical_and(tile_x(p) == x, x == b)

    def in_dev(s):
        return {"nuis": b * 8 + y * 2 + zh, "bins": 2 * s + x // 2}

    def in_is_self(s):
        return jnp.logical_and(b == x, 2 * s + x // 2 == b)

    bar = pltpu.get_barrier_semaphore()

    def greet_line(d, carry):
        pl.semaphore_signal(bar, inc=1, device_id=line_dev(d), device_id_type=MESH)
        return carry

    def greet_plane(d, carry):
        pl.semaphore_signal(bar, inc=1, device_id=plane_dev(d), device_id_type=MESH)
        return carry

    lax.fori_loop(1, 4, greet_line, 0)
    lax.fori_loop(1, PLANE, greet_plane, 0)
    for mate in (core_mate, z_mate):
        pl.semaphore_signal(bar, inc=1, device_id=mate, device_id_type=MESH)
    expected = jnp.int32(3 + PLANE - 1 + 2)
    others = [(out_dev(p), jnp.logical_and(keeps(p), jnp.logical_not(out_is_self(p)))) for p in range(4)]
    others += [(in_dev(s), jnp.logical_not(in_is_self(s))) for s in range(2)]
    for other, wanted in others:

        @pl.when(wanted)
        def _():
            pl.semaphore_signal(bar, inc=1, device_id=other, device_id_type=MESH)

        expected = expected + jnp.where(wanted, 1, 0)

    rhs_v = rhs[...]
    r_hi, r_mid = split2(rhs_v)
    r_hi, r_mid = r_hi.astype(BF16), r_mid.astype(BF16)
    pulls = rows3(pul[...])
    egs[0, 128:144, :] = jnp.zeros((16, 128), F32)

    def own_rows(i, carry):
        at = pl.ds(pl.multiple_of(i * 128, 128), 128)
        kb = lk[at, :] * mask[pl.ds(i, 1), :].astype(F32).astype(BF16)
        krow[own, at, :] = kb
        kcol[x, at, :] = kb
        e = lax.dot_general(pulls, kb, (((1,), (1,)), ((), ())), preferred_element_type=F32)
        egs[0, pl.ds(128 + i, 1), :] = e[0:1] + e[1:2] + e[2:3]
        m = jnp.dot(kb, r_hi, preferred_element_type=F32) + jnp.dot(
            kb, r_mid, preferred_element_type=F32
        )
        sb[at, :] = m.astype(BF16)

        @pl.when(i // 3 == x)
        def _():
            m1[pl.ds(pl.multiple_of((i - 3 * x) * 128, 128), 128), :] = m

        return carry

    lax.fori_loop(0, 12, own_rows, 0)

    gram = dot0(rhs_v, rhs_v, HIGHEST)
    gt[0:256, :] = gram[:, 0:128]
    gt[256:512, :] = gram[:, 128:256]
    egs[0, 0:128, :] = gt[pl.ds(pl.multiple_of(b * 128, 128), 128), :]

    pl.semaphore_wait(bar, expected)

    def line_rows(at):
        return pl.ds(pl.multiple_of(at * LINE, 16), LINE)

    def m_line(d):
        return remote(
            sb.at[line_rows((x + d) % 4)], xr.at[d - 1], g_s.at[0], g_r.at[0], line_dev(d)
        )

    def eg_line(d):
        return remote(egs.at[0], egx.at[d - 1], g_s.at[1], g_r.at[1], line_dev(d))

    for d in range(1, 4):
        eg_line(d).start()
    for d in range(1, 4):
        m_line(d).start()

    def row_copy(i, slot, to, lo=0, size=ROWS):
        ref = krow.at[slot, pl.ds(lo, size)]
        return remote(ref, ref, k_s.at[0], k_r.at[i], to)

    def col_copy(i, slot, to, lo=0, size=ROWS):
        ref = kcol.at[slot, pl.ds(lo, size)]
        return remote(ref, ref, k_s.at[1], k_r.at[i], to)

    up_x, down_x = (x + 1) % 4, (x + 3) % 4
    far_x = (x + 2) % 4
    rest = ROWS - FIRST
    copies = {
        0: (lambda: row_copy(0, own, dev(dy=1), 0, FIRST),
            lambda: row_copy(0, place(3), dev(dy=3), 0, FIRST)),
        1: (lambda: row_copy(1, own, dev(dy=3), 0, FIRST),
            lambda: row_copy(1, place(1), dev(dy=1), 0, FIRST)),
        2: (lambda: row_copy(2, own, dev(dz=1), 0, FIRST),
            lambda: row_copy(2, place(0, 1), dev(dz=1), 0, FIRST)),
        3: (lambda: col_copy(3, x, dev(dx=1), 0, HALF),
            lambda: col_copy(3, down_x, dev(dx=3), 0, HALF)),
        4: (lambda: col_copy(4, x, dev(dx=3), 0, HALF),
            lambda: col_copy(4, up_x, dev(dx=1), 0, HALF)),
        13: (lambda: row_copy(13, own, dev(dy=1), FIRST, rest),
             lambda: row_copy(13, place(3), dev(dy=3), FIRST, rest)),
        14: (lambda: row_copy(14, own, dev(dy=3), FIRST, rest),
             lambda: row_copy(14, place(1), dev(dy=1), FIRST, rest)),
        15: (lambda: row_copy(15, own, dev(dz=1), FIRST, rest),
             lambda: row_copy(15, place(0, 1), dev(dz=1), FIRST, rest)),
        16: (lambda: col_copy(16, x, dev(dx=1), HALF, HALF),
             lambda: col_copy(16, down_x, dev(dx=3), HALF, HALF)),
        17: (lambda: col_copy(17, x, dev(dx=3), HALF, HALF),
             lambda: col_copy(17, up_x, dev(dx=1), HALF, HALF)),
        5: (lambda: row_copy(5, place(3), dev(dy=1), 0, HALF),
            lambda: row_copy(5, place(2), dev(dy=3), 0, HALF)),
        6: (lambda: row_copy(6, place(1), dev(dy=3), HALF, HALF),
            lambda: row_copy(6, place(2), dev(dy=1), HALF, HALF)),
        7: (lambda: row_copy(7, place(0, 1), dev(dy=1), 0, FIRST),
            lambda: row_copy(7, place(3, 1), dev(dy=3), 0, FIRST)),
        8: (lambda: row_copy(8, place(0, 1), dev(dy=3), 0, FIRST),
            lambda: row_copy(8, place(1, 1), dev(dy=1), 0, FIRST)),
        18: (lambda: row_copy(18, place(0, 1), dev(dy=1), FIRST, rest),
             lambda: row_copy(18, place(3, 1), dev(dy=3), FIRST, rest)),
        19: (lambda: row_copy(19, place(0, 1), dev(dy=3), FIRST, rest),
             lambda: row_copy(19, place(1, 1), dev(dy=1), FIRST, rest)),
        9: (lambda: row_copy(9, place(3, 1), dev(dy=1), 0, HALF),
            lambda: row_copy(9, place(2, 1), dev(dy=3), 0, HALF)),
        10: (lambda: row_copy(10, place(1, 1), dev(dy=3), HALF, HALF),
             lambda: row_copy(10, place(2, 1), dev(dy=1), HALF, HALF)),
        11: (lambda: col_copy(11, down_x, dev(dx=1), 0, HALF),
             lambda: col_copy(11, far_x, dev(dx=3), 0, HALF)),
        12: (lambda: col_copy(12, up_x, dev(dx=3), HALF, HALF),
             lambda: col_copy(12, far_x, dev(dx=1), HALF, HALF)),
    }

    def send(*which):
        for i in which:
            copies[i][0]().start()

    def arrive(*which):
        for i in which:
            copies[i][1]().wait_recv()

    send(0, 1, 2)

    wait_all(egx, g_r.at[1])
    total = egs[0]
    for d in range(1, 4):
        total = total + egx[d - 1]
    for q in range(PLANE):
        eps[q, 0:16, :] = total[128:144]
        eps[q, 16:32, :] = total[16 * q : 16 * (q + 1)]
    wait_all(xr, g_r.at[0])
    total = m1[...]
    for d in range(1, 4):
        total = total + xr[d - 1].astype(F32)
    m1[...] = total
    send(3, 4, 16, 17)

    def m_plane(d):
        at = pl.ds(pl.multiple_of((own + d) % PLANE * SHARE, 16), SHARE)
        return remote(m1.at[at], pr.at[d], g_s.at[3], g_r.at[3], plane_dev(d))

    def e_plane(d):
        src = eps.at[(own + d) % PLANE]
        return remote(src, epr.at[d], g_s.at[4], g_r.at[4], plane_dev(d))

    def start_plane(d, carry):
        e_plane(d).start()
        m_plane(d).start()
        return carry

    lax.fori_loop(1, PLANE, start_plane, 0)
    send(13, 14, 15)

    def sum_e(d, acc):
        return acc + epr[d]

    def sum_m(d, acc):
        return acc + pr[d]

    mine = pl.ds(pl.multiple_of(x * LINE + own * SHARE, 16), SHARE)
    gram_rows = pl.ds(pl.multiple_of(own * 16, 16), 16)
    wait_all(epr.at[pl.ds(1, PLANE - 1)], g_r.at[4])
    total = lax.fori_loop(1, PLANE, sum_e, eps[own])
    egs[1, 0:32, :] = total
    g4[block, gram_rows, :] = total[16:32]
    wait_all(pr.at[pl.ds(1, PLANE - 1)], g_r.at[3])
    fb[mine, :] = lax.fori_loop(
        1, PLANE, sum_m, m1[pl.ds(pl.multiple_of(own * SHARE, 16), SHARE), :]
    ).astype(BF16)

    def m_share(d):
        return remote(fb.at[mine], fb.at[mine], g_s.at[5], g_r.at[5], plane_dev(d))

    def g_share(d):
        ref = g4.at[block, gram_rows]
        return remote(ref, ref, g_s.at[6], g_r.at[6], plane_dev(d))

    def start_share(d, carry):
        m_share(d).start()
        g_share(d).start()
        return carry

    lax.fori_loop(1, PLANE, start_share, 0)

    def yields_of(i, acc):
        at = pl.ds(pl.multiple_of(i * 128, 128), 128)
        scale = rate[proc[i]] * eff[chan[i]]
        yl = nom[pl.ds(i, 1), :] * scale * jnp.exp(egs[1, pl.ds(i, 1), :])
        ycol[at, :] = jnp.transpose(jnp.broadcast_to(yl, (128, 128)))
        return acc + jnp.dot(
            rows3(yl - obs[pl.ds(i, 1), :]), krow[own, at, :], preferred_element_type=F32
        )

    slope = lax.fori_loop(0, 12, yields_of, jnp.zeros((8, COLS), F32))
    im[0, 256:272, :] = jnp.broadcast_to(slope[0:1] + slope[1:2] + slope[2:3], (16, COLS))

    wait_all(fb.at[pl.ds(0, (PLANE - 1) * SHARE)], g_r.at[5])
    wait_all(g4.at[0, pl.ds(0, (PLANE - 1) * 16)], g_r.at[6])

    def m_all(d, at):
        ref = fb.at[line_rows(at)]
        return remote(ref, ref, g_s.at[2], g_r.at[2], line_dev(d))

    for d in range(1, 4):
        m_all(d, x).start()
    g_z = remote(g4.at[block], g4.at[block], x_s.at[6], x_r.at[6], z_mate)
    g_z.start()
    arrive(0)
    send(5)
    arrive(2)
    send(8, 7)

    def weigh(tiles):
        def step(i, carry):
            at = pl.ds(pl.multiple_of(i * 128, 128), 128)
            yl = ycol[at, :]
            yl = jnp.concatenate([yl, yl], axis=1)
            for p in tiles:
                kc = kcol[tile_x(p), at, :].astype(F32)
                wcol[at, 256 * p : 256 * (p + 1)] = (yl * kc).astype(BF16)
            return carry

        lax.fori_loop(0, 12, step, 0)

    def slot_of(k):
        j = k % 4
        return place(j + j // 2 - 2 * (j // 3), k // 4)

    def half_copy(k, p):
        return remote(pb.at[k, p], precv.at[k, p], e_s.at[p], e_r.at[k, tile_x(p) % 2], core_mate)

    def multiply(k, tiles):
        first, count = tiles[0], len(tiles)
        part = dot0(krow[slot_of(k)], wcol[:, 256 * first : 256 * (first + count)])
        for i, p in enumerate(tiles):
            pb[k, p] = part[:, 256 * i : 256 * (i + 1)]

            @pl.when(jnp.logical_not(keeps(p)))
            def _():
                half_copy(k, p).start()

    def out_slot(s, k):
        return part_o.at[s, pl.ds(pl.multiple_of(slot_of(k) * 256, 256), 256)]

    def out_copy(k, p):
        return remote(
            osend.at[k, p], out_slot(zl, k), o_s.at[p], o_r.at[zl, k], out_dev(p)
        )

    def own_copy(k, p):
        return pltpu.make_async_copy(osend.at[k, p], out_slot(zl, k), o_r.at[zl, k])

    def hand_out(k, tiles):
        for p in tiles:

            @pl.when(keeps(p))
            def _():
                half_copy(k, p).wait_recv()
                osend[k, p] = (pb[k, p] + precv[k, p]).astype(BF16)

                @pl.when(out_is_self(p))
                def _():
                    own_copy(k, p).start()

                @pl.when(jnp.logical_not(out_is_self(p)))
                def _():
                    out_copy(k, p).start()

    def each(act, blocks, tiles):
        lo, hi = blocks

        def step(k, carry):
            act(k, tiles)
            return carry

        lax.fori_loop(lo, hi, step, 0)

    weigh((0,))
    arrive(1, 13, 14)
    send(6)
    arrive(15)
    send(19, 18)


    diag, near, far, every = (0,), (1, 2), (3,), (0, 1, 2, 3)
    each(multiply, (0, 3), diag)
    each(multiply, (4, 5), diag)
    each(hand_out, (0, 3), diag)
    each(hand_out, (4, 5), diag)
    arrive(3, 4, 16, 17)
    weigh(near)
    each(multiply, (0, 3), near)
    each(multiply, (4, 5), near)

    wait_all(fb.at[pl.ds(0, 3 * LINE)], g_r.at[2])
    send(11, 12)

    def all_rows(i, carry):
        at = pl.ds(pl.multiple_of(i * 128, 128), 128)
        yl = ycol[at, :]
        vh[at, :] = (jnp.concatenate([yl, yl], axis=1) * fb[at, :].astype(F32)).astype(BF16)
        return carry

    lax.fori_loop(0, 12, all_rows, 0)
    left = dot0(fb[...], vh[:, 0:128])
    c3[0, 0:256, :] = left
    c3[0, 256:384, :] = dot0(fb[:, 128:256], vh[:, 128:256])
    c_half = pl.ds(pl.multiple_of(core * 192, 8), 192)
    i_half = pl.ds(pl.multiple_of(core * 136, 8), 136)
    c_give = pl.ds(pl.multiple_of((1 - core) * 192, 8), 192)
    i_give = pl.ds(pl.multiple_of((1 - core) * 136, 8), 136)

    def swap(buf, slot, half, sem, to):
        src = buf.at[half] if slot is None else buf.at[slot, half]
        dst = buf.at[half] if slot is None else buf.at[slot + 1, half]
        return remote(src, dst, x_s.at[sem], x_r.at[sem], to)

    c_core, c_core_in = (swap(c3, 0, h, 0, core_mate) for h in (c_give, c_half))
    i_core, i_core_in = (swap(im, 0, h, 1, core_mate) for h in (i_give, i_half))
    c_z, i_z = swap(c3, 2, c_half, 2, z_mate), swap(im, 2, i_half, 3, z_mate)
    c_all, c_all_in = (swap(ctot, None, h, 4, core_mate) for h in (c_half, c_give))
    i_all, i_all_in = (swap(itot, None, h, 5, core_mate) for h in (i_half, i_give))
    c_core.start()
    im[0, 0:256, :] = dot0(wcol[:, 0:256], fb[...])
    i_core.start()
    mate = pl.ds((1 - core) * 2, 2)
    pair = pl.ds(core * 2, 2)
    g_z_in = remote(g4.at[core * 2 + 1 - zl], g4.at[core * 2 + 1 - zl], x_s.at[6], x_r.at[6], z_mate)
    g_all = remote(g4.at[pair], g4.at[pair], x_s.at[7], x_r.at[7], core_mate)
    g_all_in = remote(g4.at[mate], g4.at[mate], x_s.at[7], x_r.at[7], core_mate)
    g_z_in.wait_recv()
    g_all.start()

    c_core_in.wait_recv()
    c3[2, c_half, :] = c3[0, c_half, :] + c3[1, c_half, :]
    c_z.start()
    i_core_in.wait_recv()
    im[2, i_half, :] = im[0, i_half, :] + im[1, i_half, :]
    i_z.start()

    c_z.wait_recv()
    ctot[c_half, :] = c3[2, c_half, :] + c3[3, c_half, :]
    c_all.start()
    each(hand_out, (0, 3), near)
    each(hand_out, (4, 5), near)
    c_all_in.wait_recv()
    g_all_in.wait_recv()
    total = ctot[...]
    ab[0:128, 0:128] = total[0:128] + g4[0]
    ab[128:256, 0:128] = total[128:256] + g4[2]
    ab[0:128, 128:256] = jnp.transpose(total[128:256]) + g4[1]
    ab[128:256, 128:256] = total[256:384] + g4[3]
    for i in range(4):
        row, col = 128 * (i // 2), 256 + 128 * (i % 2)
        ab[row : row + 128, col : col + 128] = g4[i]

    def eliminate(i, carry):
        pivot = invert(ab[0:PIV, 0:PIV])
        head = jnp.dot(pivot, ab[0:PIV, :], preferred_element_type=F32, precision=HIGHEST)
        rest = ab[PIV:256, :] - jnp.dot(
            ab[PIV:256, 0:PIV], head, preferred_element_type=F32, precision=HIGHEST
        )
        ab[0 : 256 - PIV, 0:256] = pltpu.roll(rest[:, 0:256], 256 - PIV, 1)
        ab[0 : 256 - PIV, 256:512] = rest[:, 256:512]
        ab[256 - PIV : 256, 0:256] = pltpu.roll(head[:, 0:256], 256 - PIV, 1)
        ab[256 - PIV : 256, 256:512] = head[:, 256:512]
        return carry

    lax.fori_loop(0, 2, eliminate, 0)
    arrive(7)
    send(9)
    arrive(8, 19)
    send(10)
    arrive(11, 12)
    weigh(far)
    each(multiply, (0, 3), far)
    each(multiply, (4, 5), far)
    each(hand_out, (0, 3), far)
    each(hand_out, (4, 5), far)
    arrive(5, 6)
    each(multiply, (3, 4), every)
    arrive(18)
    each(multiply, (5, 7), every)
    each(hand_out, (3, 4), every)
    each(hand_out, (5, 7), every)
    i_z.wait_recv()
    itot[i_half, :] = im[2, i_half, :] + im[3, i_half, :]
    i_all.start()
    lax.fori_loop(2, 3, eliminate, 0)
    arrive(9, 10)
    each(multiply, (7, 8), every)
    each(hand_out, (7, 8), every)
    lax.fori_loop(3, 4, eliminate, 0)
    step = ab[:, 256:512]
    imp_v[...] = jnp.dot(rhs_v, step, preferred_element_type=F32, precision=HIGHEST)
    results = [
        pltpu.make_async_copy(grad_v, grad_o, w_s.at[0]),
        pltpu.make_async_copy(imp_v, imp_o, w_s.at[1]),
        pltpu.make_async_copy(res_v, res_o, w_s.at[2]),
    ]
    results[1].start()
    i_all_in.wait_recv()
    grad_v[...] = itot[256:257, :] + pul[...]
    results[0].start()
    image = rhs_v + itot[0:256, :]
    res_v[...] = rhs_v - jnp.dot(image, step, preferred_element_type=F32, precision=HIGHEST)
    results[2].start()

    def finish(k, carry):
        for s in range(2):
            ref = out_slot(s, k)
            pltpu.make_async_copy(ref, ref, o_r.at[s, k]).wait()
        return carry

    lax.fori_loop(0, 8, finish, 0)

    wait_all(xr, g_s.at[0])
    wait_all(egx, g_s.at[1])
    wait_all(fb.at[pl.ds(0, 3 * LINE)], g_s.at[2])
    wait_all(pr.at[pl.ds(1, PLANE - 1)], g_s.at[3])
    wait_all(epr.at[pl.ds(1, PLANE - 1)], g_s.at[4])
    wait_all(fb.at[pl.ds(0, (PLANE - 1) * SHARE)], g_s.at[5])
    wait_all(g4.at[0, pl.ds(0, (PLANE - 1) * 16)], g_s.at[6])
    wait_all(krow.at[pl.ds(0, 7)], k_s.at[0])
    wait_all(kcol.at[pl.ds(0, 3)], k_s.at[1])
    for copy in (c_core, c_z, c_all, i_core, i_z, i_all, g_z, g_all):
        copy.wait_send()

    for p in range(4):

        @pl.when(jnp.logical_not(keeps(p)))
        def _():
            wait_all(pb.at[:, p], e_s.at[p])

        @pl.when(jnp.logical_and(keeps(p), jnp.logical_not(out_is_self(p))))
        def _():
            wait_all(osend.at[:, p], o_s.at[p])

    for copy in results:
        copy.wait()


def body(
    log_kappa, block_mask, process, channel, nominal, observed, process_rate, efficiency,
    nuisance_pulls, impact_rhs,
):
    vmem = pl.BlockSpec(memory_space=pltpu.VMEM)
    smem = pl.BlockSpec(memory_space=pltpu.SMEM)
    dma = pltpu.SemaphoreType.DMA
    gradient, parts, impacts, residual = pl.pallas_call(
        kernel,
        name="gauss_newton",
        out_shape=(
            jax.ShapeDtypeStruct((1, COLS), F32),
            jax.ShapeDtypeStruct((2, 2048, COLS), BF16),
            jax.ShapeDtypeStruct((256, 256), F32),
            jax.ShapeDtypeStruct((256, 256), F32),
        ),
        in_specs=[vmem] * 6 + [smem] * 4,
        out_specs=(pl.BlockSpec(memory_space=pl.ANY),) * 4,
        scratch_shapes=[
            pltpu.VMEM((8, ROWS, COLS), BF16),
            pltpu.VMEM((4, ROWS, COLS), BF16),
            pltpu.VMEM((ROWS, 1024), BF16),
            pltpu.VMEM((ROWS, COLS), BF16),
            pltpu.VMEM((3, LINE, COLS), BF16),
            pltpu.VMEM((LINE, COLS), F32),
            pltpu.VMEM((PLANE, SHARE, COLS), F32),
            pltpu.VMEM((ROWS, COLS), BF16),
            pltpu.VMEM((ROWS, 128), F32),
            pltpu.VMEM((ROWS, COLS), BF16),
            pltpu.VMEM((512, 128), F32),
            pltpu.VMEM((4, 128, 128), F32),
            pltpu.VMEM((2, 144, 128), F32),
            pltpu.VMEM((3, 144, 128), F32),
            pltpu.VMEM((PLANE, 32, 128), F32),
            pltpu.VMEM((PLANE, 32, 128), F32),
            pltpu.VMEM((4, 384, 128), F32),
            pltpu.VMEM((4, 272, COLS), F32),
            pltpu.VMEM((256, 512), F32),
            pltpu.VMEM((8, 4, 256, 256), F32),
            pltpu.VMEM((8, 4, 256, 256), F32),
            pltpu.VMEM((8, 4, 256, 256), BF16),
            pltpu.VMEM((384, 128), F32),
            pltpu.VMEM((272, COLS), F32),
            pltpu.VMEM((1, COLS), F32),
            pltpu.VMEM((256, 256), F32),
            pltpu.VMEM((256, 256), F32),
            dma((7,)), dma((7,)), dma((2,)), dma((20,)), dma((8,)), dma((8,)), dma((3,)),
            dma((4,)), dma((8, 2)), dma((4,)), dma((2, 8)),
        ],
        compiler_params=pltpu.CompilerParams(
            collective_id=0, has_side_effects=True, vmem_limit_bytes=62 * 2**20
        ),
    )(
        log_kappa, block_mask, nominal.reshape(12, 128), observed.reshape(12, 128),
        nuisance_pulls.reshape(1, COLS), impact_rhs, process, channel, process_rate, efficiency,
    )
    tile_rows = 8 * 256
    row = lax.axis_index("bins") * tile_rows + lax.broadcasted_iota(jnp.int32, (tile_rows, COLS), 0)
    col = lax.axis_index("nuis") * COLS + lax.broadcasted_iota(jnp.int32, (tile_rows, COLS), 1)
    first, second = (parts[s].astype(F32) for s in range(2))
    hessian = first + second + (row == col).astype(F32)
    return gradient.reshape(COLS), hessian, impacts, residual


def solution(mesh):
    in_specs = (
        P("bins", "nuis"),
        P("bins", "nuis"),
        P("bins"),
        P("bins"),
        P("bins"),
        P("bins"),
        P(),
        P(),
        P("nuis"),
        P("nuis", None),
    )
    out_specs = (P("nuis"), P("bins", "nuis"), P("nuis", None), P("nuis", None))
    return jax.shard_map(body, mesh=mesh, in_specs=in_specs, out_specs=out_specs, check_vma=False)
```
